256 devices in a mesh: dp: 16 (over z, core), group: 16 (over x, y).
Axes of the slice: x: 4, y: 4, z: 8, core: 2. Of those that a mesh axis runs over, the one named last changes fastest.
Arguments:
- features: bfloat16 [524288, 512], P(('dp', 'group')), parts along dimension 0, may hold values from -36.2 to 36.2
- proj_weight: bfloat16 [512, 256], replicated, may hold values from -0.25 to 0.25
- class_weight: bfloat16 [8192, 124], P('dp'), parts along dimension 0, may hold values from -0.1777767 to 0.1777767
- anchor_blocks: int32 [256], P('dp'), parts along dimension 0, may hold values from 1 to 4, as said below
- anchor_pix: int32 [256, 512], P(('dp', 'group')), parts along dimension 0, may hold values from 0 to 2047, as said below
- anchor_label: int32 [256, 512], P('dp'), parts along dimension 0, may hold values from 0 to 123
- pixel_label: int32 [524288], P(('dp', 'group')), parts along dimension 0, may hold values from 0 to 123
Outputs:
- grad_features: bfloat16 [524288, 512], P(('dp', 'group')), parts along dimension 0
- grad_proj: float32 [8192, 256], P('dp'), parts along dimension 0
- grad_class: float32 [8192, 124], P('dp'), parts along dimension 0
- losses: float32 [32], P('dp'), parts along dimension 0
The draws below stay inside these ranges and needn't reach their ends.
There are 16 independent parts, one for each index of `dp`. The reference program is written for one: setup_inputs(seed, part) draws one part's arguments, and reference() takes and returns one part's arrays. A program takes and returns all parts, laid end to end along the dimension named above; an argument that names none is the same for every part. Nothing has to cross between parts.
Inputs may be any that keep to these rules, and one draw needn't show every extreme that they name: Anchor rows of image g at slots 128 * anchor_blocks[g] and beyond are unused. `anchor_pix`: within one image the pixel indices of the slots are distinct.
All inputs are finite; a program needn't handle non-finite values.
Results may differ from the reference program's by a relative error of at most 0.0037.
Values may be sent and summed in bfloat16 or wider, within the bound.
No kernel may reach another device: no remote copies, remote signals or barrier semaphores. Data moves between devices by JAX's collectives and lax.ppermute only.
A program may use at most 128 MiB of HBM per device.

```python
import math
import jax
import jax.numpy as jnp
import numpy as np
from jax import lax

CIN = 512
EMB = 256
NCLS = 124
PIX = 2048
BLK = 128
MAXB = 4
MAXA = 512
ALL_PIX = 32768
N_GROUP = 16


prototype_total = 16


def draw_class_weight(key, part):
    key = jax.random.fold_in(key, 11)
    table = jnp.clip(jax.random.normal(key, (CIN, NCLS), jnp.float32), -4.0, 4.0)
    return (table * CIN ** (-0.5)).astype(jnp.bfloat16)


def prototype_rows(key):
    key_proto, key_main, key_pick, key_member = jax.random.split(key, 4)
    prototypes = jnp.where(jax.random.bernoulli(key_proto, 0.5, (prototype_total, CIN)), 1.0, -1.0).astype(jnp.float32)
    dominant = jax.random.randint(key_main, (), 0, prototype_total)
    spread_ids = jax.random.randint(key_member, (ALL_PIX,), 0, prototype_total)
    member = jnp.where(jax.random.randint(key_pick, (ALL_PIX,), 0, 5) < 2, dominant, spread_ids)
    return prototypes[member]


def draw_features(key, part):
    key = jax.random.fold_in(key, 12)
    key_base = jax.random.fold_in(key, 0)
    key_cluster = jax.random.fold_in(key, 4)
    cluster_rows = 1.5 * prototype_rows(key_cluster)
    values = jnp.clip(jax.random.normal(key_base, (ALL_PIX, CIN), jnp.float32) + cluster_rows, -6.0, 6.0)
    return values.astype(jnp.bfloat16)


def draw_anchor_blocks(key, part):
    key = jax.random.fold_in(key, 13)
    key_law, key_top, key_low = jax.random.split(key, 3)
    drawn = jax.random.randint(key_law, (N_GROUP,), 0, 16)
    blocks = 1 + (drawn >= 10).astype(jnp.int32) + (drawn >= 13).astype(jnp.int32) + (drawn >= 15).astype(jnp.int32)
    blocks = jnp.minimum(blocks, MAXB)
    busiest = jax.random.randint(key_top, (), 0, N_GROUP)
    lightest = (busiest + 1 + jax.random.randint(key_low, (), 0, N_GROUP - 1)) % N_GROUP
    group_ids = jnp.arange(N_GROUP, dtype=jnp.int32)
    blocks = jnp.where(group_ids == busiest, MAXB, blocks)
    blocks = jnp.where(group_ids == lightest, 1, blocks)
    return blocks.astype(jnp.int32)


def draw_anchor_pix(key, part):
    key = jax.random.fold_in(key, 14)
    image_keys = jax.random.split(key, N_GROUP)

    def one_image(image_key):
        order = jax.random.permutation(image_key, PIX).astype(jnp.int32)
        top_place = jnp.argmax(order == PIX - 1)
        order = order.at[top_place].set(order[0]).at[0].set(PIX - 1)
        low_place = jnp.argmax(order == 0)
        order = order.at[low_place].set(order[1]).at[1].set(0)
        return order[:MAXA]
    return jax.vmap(one_image)(image_keys).astype(jnp.int32)


def touch_ends(result, own_key, smallest, high):
    dims = result.shape
    index_at = [jax.random.randint(jax.random.fold_in(own_key, axis), (), 0, dims[axis]) for axis in range(len(dims))]
    result = result.at[tuple(index_at)].set(smallest)
    longest = dims.index(max(dims))
    index_at[longest] = (index_at[longest] + 1) % dims[longest]
    return result.at[tuple(index_at)].set(high)


def cumulative_ranks(amount, lean):
    loads = [(1 << 20) // math.isqrt(standing ** lean) + 1 for standing in range(1, amount + 1)]
    width = 1 + sum(loads) // (1 << 30)
    return np.cumsum(np.array([max(1, weight // width) for weight in loads]))


def ranked(rng, shape, number_of, slope):
    listing = cumulative_ranks(number_of, slope)
    ticket = jax.random.randint(jax.random.fold_in(rng, 1), shape, 0, int(listing[number_of - 1]))
    grade = jnp.searchsorted(jnp.asarray(listing, jnp.int32), ticket, side="right")
    return jax.random.permutation(jax.random.fold_in(rng, 2), number_of)[grade].astype(jnp.int32)


def gaussian(own_key, dims, deviation, most, held_as=jnp.bfloat16):
    return jnp.clip(deviation * jax.random.normal(own_key, dims, jnp.float32), -most, most).astype(held_as)


def setup_inputs(seed: int = 0, part: int = 0) -> dict:
    keys = jax.random.split(jax.random.key(seed), 8)
    part_keys = jax.random.split(jax.random.fold_in(keys[7], part), 8)
    features = draw_features(jax.random.fold_in(jax.random.fold_in(keys[7], part), 71), part)
    proj_weight = gaussian(keys[1], (CIN, EMB), CIN ** -0.5, 0.25)
    class_weight = draw_class_weight(jax.random.fold_in(jax.random.fold_in(keys[7], part), 71), part)
    anchor_blocks = draw_anchor_blocks(jax.random.fold_in(jax.random.fold_in(keys[7], part), 71), part)
    anchor_pix = draw_anchor_pix(jax.random.fold_in(jax.random.fold_in(keys[7], part), 71), part)
    anchor_label = touch_ends(ranked(part_keys[5], (N_GROUP, MAXA), NCLS, 2), jax.random.fold_in(part_keys[5], 3), 0, NCLS - 1).astype(jnp.int32)
    pixel_label = touch_ends(ranked(part_keys[6], (ALL_PIX,), NCLS, 1), jax.random.fold_in(part_keys[6], 3), 0, NCLS - 1).astype(jnp.int32)
    return {"features": features, "proj_weight": proj_weight, "class_weight": class_weight, "anchor_blocks": anchor_blocks, "anchor_pix": anchor_pix, "anchor_label": anchor_label, "pixel_label": pixel_label}


INV_TEMP = 10.0
CONTRAST_WEIGHT = 0.1
NORM_EPS = 1e-06

def pair_scores(left, right):
    return lax.dot_general(left, right, (((1,), (1,)), ((), ())), preferred_element_type=jnp.float32)

def column_sum(left, right):
    return lax.dot_general(left, right, (((0,), (0,)), ((), ())), preferred_element_type=jnp.float32)

def exact_pair(left, right):
    return lax.dot_general(left, right, (((1,), (1,)), ((), ())), precision=lax.Precision.HIGHEST, preferred_element_type=jnp.float32)

def exact_column(left, right):
    return lax.dot_general(left, right, (((0,), (0,)), ((), ())), precision=lax.Precision.HIGHEST, preferred_element_type=jnp.float32)

def row_terms(queries, row_ids, query_labels, query_keep, key_rows, key_labels, key_keep):
    scores = pair_scores(queries, key_rows) * INV_TEMP
    column_ids = jnp.arange(key_rows.shape[0], dtype=jnp.int32)
    allowed = key_keep[None, :] & (column_ids[None, :] != row_ids[:, None])
    totals = lax.optimization_barrier(jnp.sum(jnp.where(allowed, jnp.exp(scores - INV_TEMP), 0.0), axis=1))
    logsum = jnp.log(totals) + INV_TEMP
    same_mask = (allowed & (query_labels[:, None] == key_labels[None, :])).astype(jnp.float32)
    pos_count = lax.optimization_barrier(jnp.sum(same_mask, axis=1))
    pos_floor = jnp.maximum(pos_count, 1.0)
    keep_float = query_keep.astype(jnp.float32)
    anchor_loss = keep_float * (pos_count * logsum - lax.optimization_barrier(jnp.sum(same_mask * scores, axis=1))) / pos_floor
    return (scores, allowed, same_mask, logsum, pos_count, keep_float, anchor_loss)

def coefficients(scores, allowed, same_mask, logsum, pos_count, keep_float):
    pos_floor = jnp.maximum(pos_count, 1.0)
    pos_ratio = pos_count / pos_floor
    probable = jnp.where(allowed, jnp.exp(scores - logsum), 0.0)
    scaled = CONTRAST_WEIGHT * INV_TEMP * keep_float * (pos_ratio * probable - same_mask / pos_floor)
    return scaled.astype(jnp.bfloat16)

def reference(features, proj_weight, class_weight, anchor_blocks, anchor_pix, anchor_label, pixel_label):
    groups, slot_count = anchor_pix.shape
    pixel_count = features.shape[0] // groups
    channels = features.shape[1]
    images = features.reshape(groups, pixel_count, channels)
    picked = jax.vmap(lambda one_image, pix_ids: one_image[pix_ids])(images, anchor_pix)
    picked = picked.reshape(groups * slot_count, channels)
    projected = jnp.dot(picked, proj_weight, preferred_element_type=jnp.float32)
    length = jnp.sqrt(lax.optimization_barrier(jnp.sum(projected * projected, axis=1, keepdims=True)) + NORM_EPS)
    unit_rows = projected / length
    embedded = unit_rows.astype(jnp.bfloat16)
    row_limit = jnp.broadcast_to((anchor_blocks * BLK)[:, None], (groups, slot_count)).reshape(-1)
    slot_ids = jnp.broadcast_to(jnp.arange(slot_count, dtype=jnp.int32)[None, :], (groups, slot_count)).reshape(-1)
    keep_mask = slot_ids < row_limit
    label_rows = anchor_label.reshape(-1)
    total_rows = groups * slot_count

    def visit_block(loop_state, block_id):
        key_grad, contrast_sum = loop_state
        row_start = block_id * BLK
        queries = lax.dynamic_slice_in_dim(embedded, row_start, BLK, 0)
        row_ids = row_start + jnp.arange(BLK, dtype=jnp.int32)
        query_labels = lax.dynamic_slice_in_dim(label_rows, row_start, BLK, 0)
        query_keep = lax.dynamic_slice_in_dim(keep_mask, row_start, BLK, 0)
        scores, allowed, same_mask, logsum, pos_count, keep_float, anchor_loss = row_terms(queries, row_ids, query_labels, query_keep, embedded, label_rows, keep_mask)
        coefficient = coefficients(scores, allowed, same_mask, logsum[:, None], pos_count[:, None], keep_float[:, None])
        row_grad = jnp.dot(coefficient, embedded, preferred_element_type=jnp.float32)
        key_grad = key_grad + column_sum(coefficient, queries)
        return ((key_grad, contrast_sum + jnp.sum(anchor_loss)), row_grad)
    start_state = (jnp.zeros((total_rows, embedded.shape[1]), jnp.float32), jnp.zeros((), jnp.float32))
    (key_grad, contrast_sum), row_grads = lax.scan(visit_block, start_state, jnp.arange(total_rows // BLK, dtype=jnp.int32))
    grad_embedded = key_grad + row_grads.reshape(total_rows, -1)
    radial = lax.optimization_barrier(jnp.sum(unit_rows * grad_embedded, axis=1, keepdims=True))
    grad_projected = (grad_embedded - unit_rows * radial) / length
    grad_proj = exact_column(picked.astype(jnp.float32), grad_projected)
    grad_picked = exact_pair(grad_projected, proj_weight.astype(jnp.float32))
    logits = jnp.dot(features, class_weight, preferred_element_type=jnp.float32)
    top_logit = lax.optimization_barrier(jnp.max(logits, axis=1, keepdims=True))
    logsum_class = jnp.log(lax.optimization_barrier(jnp.sum(jnp.exp(logits - top_logit), axis=1, keepdims=True))) + top_logit
    onehot = (pixel_label[:, None] == jnp.arange(logits.shape[1], dtype=jnp.int32)[None, :]).astype(jnp.float32)
    pixel_loss = logsum_class[:, 0] - lax.optimization_barrier(jnp.sum(onehot * logits, axis=1))
    grad_logits = (jnp.exp(logits - logsum_class) - onehot).astype(jnp.bfloat16)
    grad_class = column_sum(features, grad_logits)
    from_classes = pair_scores(grad_logits, class_weight)
    scattered = jax.vmap(lambda pix_ids, grad_rows: jnp.zeros((pixel_count, channels), jnp.float32).at[pix_ids].add(grad_rows))(anchor_pix, grad_picked.reshape(groups, slot_count, channels))
    grad_features = (from_classes + scattered.reshape(groups * pixel_count, channels)).astype(jnp.bfloat16)
    losses = jnp.stack([jnp.sum(pixel_loss) / float(groups * pixel_count), contrast_sum / jnp.sum(keep_mask.astype(jnp.float32))])
    return (grad_features, grad_proj, grad_class, losses)
```

```python
import jax
import jax.numpy as jnp
from jax import lax
from jax.experimental import pallas as pl
from jax.experimental.pallas import tpu as pltpu
from jax.sharding import PartitionSpec as P

BLK = 128
TILE = 512
INV_TEMP = 10.0
LOG2E = 1.4426950408889634
EXP_SCALE = INV_TEMP * LOG2E
NORM_EPS = 1e-06
VMEM_BYTES = 40 * 1024 * 1024

NT = (((1,), (1,)), ((), ()))
TN = (((0,), (0,)), ((), ()))


def dot_f32(left, right, dims):
    return lax.dot_general(left, right, dims, preferred_element_type=jnp.float32)


def split_bf16(value):
    high = value.astype(jnp.bfloat16)
    rest = value - high.astype(jnp.float32)
    middle = rest.astype(jnp.bfloat16)
    low = (rest - middle.astype(jnp.float32)).astype(jnp.bfloat16)
    return high, middle, low


def load_keys(plan_ref, keys_hbm, keys, sem):
    valid = plan_ref[64]
    tiles = (valid * BLK + TILE - 1) // TILE

    def copy_of(place):
        return pltpu.make_async_copy(
            keys_hbm.at[pl.ds(pl.multiple_of(plan_ref[place] * BLK, BLK), BLK)],
            keys.at[pl.ds(pl.multiple_of(place * BLK, BLK), BLK)],
            sem,
        )

    def begin(place, carry):
        copy_of(place).start()
        return carry

    def end(place, carry):
        copy_of(place).wait()
        return carry

    def clear(place, carry):
        keys[pl.ds(pl.multiple_of(place * BLK, BLK), BLK), :] = jnp.zeros(
            (BLK, keys.shape[1]), keys.dtype
        )
        return carry

    lax.fori_loop(0, valid, begin, 0)
    lax.fori_loop(valid, tiles * (TILE // BLK), clear, 0)
    lax.fori_loop(0, valid, end, 0)
    return tiles


def own_diagonal(plan_ref, tile, block):
    rows = lax.broadcasted_iota(jnp.int32, (BLK, TILE), 0)
    cols = lax.broadcasted_iota(jnp.int32, (BLK, TILE), 1)
    return cols - rows == (plan_ref[65] + block) * BLK - tile * TILE


def fold_lanes(value):
    total = value[:, :BLK]
    for start in range(BLK, value.shape[1], BLK):
        total = total + value[:, start : start + BLK]
    return total


def sums_kernel(plan_ref, own_ref, bias_ref, keys_hbm, acc_ref, sums_ref, keys, sem):
    tiles = load_keys(plan_ref, keys_hbm, keys, sem)
    blocks = own_ref.shape[0] // BLK
    acc_ref[...] = jnp.zeros_like(acc_ref)

    def visit(tile, carry):
        span = pl.ds(pl.multiple_of(tile * TILE, TILE), TILE)
        key_tile = keys[span, :]
        bias = bias_ref[:, span]
        for block in range(blocks):
            rows = slice(block * BLK, (block + 1) * BLK)
            scores = dot_f32(own_ref[rows, :], key_tile, NT)
            weights = jnp.exp2(scores * EXP_SCALE + bias)
            weights = jnp.where(own_diagonal(plan_ref, tile, block), 0.0, weights)
            acc_ref[rows, :] += fold_lanes(weights)
        return carry

    lax.fori_loop(0, tiles, visit, 0)
    for block in range(blocks):
        rows = slice(block * BLK, (block + 1) * BLK)
        sums_ref[block : block + 1, :] = jnp.sum(acc_ref[rows, :].T, axis=0, keepdims=True)


def rows_kernel(
    plan_ref, own_ref, info_ref, acc_ref, label_ref, keys_hbm, grad_ref, loss_ref, keys, same_acc, sem
):
    tiles = load_keys(plan_ref, keys_hbm, keys, sem)
    blocks = own_ref.shape[0] // BLK
    grad_ref[...] = jnp.zeros_like(grad_ref)
    same_acc[...] = jnp.zeros_like(same_acc)
    keep = info_ref[:, 0:1]
    own_label = info_ref[:, 1:2]
    pos_count = info_ref[:, 2:3]
    pos_floor = jnp.maximum(pos_count, 1.0)
    total = jnp.sum(acc_ref[...], axis=1, keepdims=True)
    row_scale = keep * (pos_count / pos_floor) / total
    pos_scale = keep / pos_floor

    def visit(tile, carry):
        span = pl.ds(pl.multiple_of(tile * TILE, TILE), TILE)
        key_tile = keys[span, :]
        key_label = label_ref[:, span]
        for block in range(blocks):
            rows = slice(block * BLK, (block + 1) * BLK)
            scores = dot_f32(own_ref[rows, :], key_tile, NT)
            diagonal = own_diagonal(plan_ref, tile, block)
            weights = jnp.exp2(scores * EXP_SCALE - EXP_SCALE)
            same = (own_label[rows] == key_label) & ~diagonal
            weights = jnp.where(diagonal, 0.0, weights)
            part = row_scale[rows] * weights
            coefficient = jnp.where(same, part - pos_scale[rows], part).astype(jnp.bfloat16)
            same_acc[rows, :] += fold_lanes(jnp.where(same, scores, 0.0))
            grad_ref[rows, :] += jnp.dot(
                coefficient, key_tile, preferred_element_type=jnp.float32
            )
        return carry

    lax.fori_loop(0, tiles, visit, 0)
    same_sum = INV_TEMP * jnp.sum(same_acc[...], axis=1, keepdims=True)
    logsum = jnp.log(total) + INV_TEMP
    loss = keep * (pos_count * logsum - same_sum) / pos_floor
    loss_ref[...] = jnp.broadcast_to(jnp.sum(loss, axis=0, keepdims=True), loss_ref.shape)


def keys_kernel(
    plan_ref,
    own_ref,
    info_ref,
    label_ref,
    ratio_ref,
    floor_ref,
    sums_ref,
    row_grad_ref,
    unit_ref,
    length_ref,
    picked_ref,
    class_ref,
    keys_hbm,
    grad_ref,
    out_ref,
    keys,
    scale,
    acc,
    sem,
):
    valid = plan_ref[64]
    tiles = load_keys(plan_ref, keys_hbm, keys, sem)
    blocks = own_ref.shape[0] // BLK
    scale[...] = jnp.ones_like(scale)

    def place_sums(place, carry):
        span = pl.ds(pl.multiple_of(place * BLK, BLK), BLK)
        scale[:, span] = sums_ref[pl.ds(plan_ref[place], 1), :]
        return carry

    lax.fori_loop(0, valid, place_sums, 0)
    acc[...] = row_grad_ref[...]
    keep = info_ref[:, 0:1]
    own_label = info_ref[:, 1:2]

    def visit(tile, carry):
        span = pl.ds(pl.multiple_of(tile * TILE, TILE), TILE)
        key_tile = keys[span, :]
        key_label = label_ref[:, span]
        key_scale = ratio_ref[:, span] / scale[:, span]
        key_floor = floor_ref[:, span]
        for block in range(blocks):
            rows = slice(block * BLK, (block + 1) * BLK)
            scores = dot_f32(own_ref[rows, :], key_tile, NT)
            diagonal = own_diagonal(plan_ref, tile, block)
            part = key_scale * jnp.exp2(scores * EXP_SCALE - EXP_SCALE)
            part = jnp.where(own_label[rows] == key_label, part - key_floor, part)
            part = jnp.where(diagonal, 0.0, part) * keep[rows]
            acc[rows, :] += jnp.dot(
                part.astype(jnp.bfloat16), key_tile, preferred_element_type=jnp.float32
            )
        return carry

    lax.fori_loop(0, tiles, visit, 0)
    unit = unit_ref[...]
    grad = acc[...]
    radial = jnp.sum(unit * grad, axis=1, keepdims=True)
    grad = (grad - unit * radial) / length_ref[...]
    grad_ref[...] = grad
    high, middle, low = split_bf16(grad)
    picked = picked_ref[...]
    width = grad.shape[1]
    out_ref[:, :width] = (
        dot_f32(picked, high, TN) + dot_f32(picked, middle, TN) + dot_f32(picked, low, TN)
    )
    out_ref[:, width:] = class_ref[...]


def in_vmem(count):
    return [pl.BlockSpec(memory_space=pltpu.VMEM)] * count


def run(kernel, name, out_shape, scratch, plan, arrays, keys, cost):
    return pl.pallas_call(
        kernel,
        name=name,
        out_shape=out_shape,
        in_specs=[pl.BlockSpec(memory_space=pltpu.SMEM)]
        + in_vmem(len(arrays))
        + [pl.BlockSpec(memory_space=pl.ANY)],
        out_specs=in_vmem(len(out_shape)),
        scratch_shapes=[pltpu.VMEM(keys.shape, keys.dtype)] + scratch + [pltpu.SemaphoreType.DMA],
        compiler_params=pltpu.CompilerParams(vmem_limit_bytes=VMEM_BYTES),
        cost_estimate=cost,
    )(plan, *arrays, keys)


def to_all(value, groups):
    copies = jnp.broadcast_to(value[None], (groups,) + value.shape)
    return lax.all_to_all(copies, "group", 0, 0, tiled=True)


def per_device(
    features, proj_weight, class_weight, anchor_blocks, anchor_pix, anchor_label, pixel_label
):
    groups = lax.axis_size("group")
    me = lax.axis_index("group")
    slots = anchor_pix.shape[1]
    pixels, channels = features.shape
    classes = class_weight.shape[1]
    width = proj_weight.shape[1]
    per_image = slots // BLK
    blocks = groups * per_image
    f32 = jnp.float32

    pix_ids = anchor_pix[0]
    picked = features[pix_ids]
    projected = jnp.dot(picked, proj_weight, preferred_element_type=f32)
    length = jnp.sqrt(jnp.sum(projected * projected, axis=1, keepdims=True) + NORM_EPS)
    unit = projected / length
    embedded = unit.astype(jnp.bfloat16)
    keys = to_all(embedded, groups).reshape(groups * slots, width)

    block_ids = jnp.arange(blocks, dtype=jnp.int32)
    block_valid = (block_ids % per_image) < jnp.repeat(
        anchor_blocks, per_image, total_repeat_length=blocks
    )
    ranks = jnp.cumsum(block_valid.astype(jnp.int32)) - 1
    valid = jnp.sum(block_valid.astype(jnp.int32))
    chosen = block_valid[None, :] & (ranks[None, :] == block_ids[:, None])
    order = jnp.sum(jnp.where(chosen, block_ids[None, :], 0), axis=1)
    is_mine = jnp.arange(groups, dtype=jnp.int32) == me
    before = jnp.sum(jnp.where(jnp.arange(groups, dtype=jnp.int32) < me, anchor_blocks, 0))
    plan = jnp.concatenate([order, valid[None], before[None]]).astype(jnp.int32)
    labels = anchor_label.reshape(blocks, BLK)
    label_ids = jnp.arange(classes, dtype=jnp.int32)
    onehot_labels = (labels[:, :, None] == label_ids).astype(f32)
    histogram = jnp.sum(onehot_labels * block_valid[:, None, None].astype(f32), axis=(0, 1))
    pos_count = jnp.sum(onehot_labels * histogram, axis=2) - 1.0
    pos_count = jnp.where(block_valid[:, None], pos_count, 0.0)
    pos_floor = jnp.maximum(pos_count, 1.0)
    in_use = (block_ids < valid)[:, None]
    label_f = labels.astype(f32)
    key_labels = jnp.where(in_use, label_f[order], -1.0).reshape(1, -1)
    key_ratio = jnp.where(in_use, (pos_count / pos_floor)[order], 0.0).reshape(1, -1)
    key_floor = jnp.where(in_use, (1.0 / pos_floor)[order], 0.0).reshape(1, -1)
    key_bias = jnp.where(key_labels >= 0.0, -EXP_SCALE, -1e30)

    def own_rows(value):
        per = value.reshape(groups, slots)
        return jnp.sum(jnp.where(is_mine[:, None], per, 0.0), axis=0)

    keep_rows = jnp.broadcast_to(block_valid.astype(f32)[:, None], (blocks, BLK))
    info = jnp.stack([own_rows(keep_rows), own_rows(label_f), own_rows(pos_count)], axis=1)

    logits = jnp.dot(features, class_weight, preferred_element_type=f32)
    top_logit = jnp.max(logits, axis=1, keepdims=True)
    logsum_class = jnp.log(jnp.sum(jnp.exp(logits - top_logit), axis=1, keepdims=True)) + top_logit
    onehot = (pixel_label[:, None] == label_ids[None, :]).astype(f32)
    pixel_loss = logsum_class[:, 0] - jnp.sum(onehot * logits, axis=1)
    grad_logits = (jnp.exp(logits - logsum_class) - onehot).astype(jnp.bfloat16)
    class_part = dot_f32(features, grad_logits, TN)
    from_classes = dot_f32(grad_logits, class_weight, NT)

    pairs = slots * groups * slots
    acc, own_sums = run(
        sums_kernel,
        "anchor_sums",
        [jax.ShapeDtypeStruct((slots, BLK), f32), jax.ShapeDtypeStruct((per_image, BLK), f32)],
        [],
        plan,
        [embedded, key_bias],
        keys,
        pl.CostEstimate(flops=pairs * width, bytes_accessed=2 * keys.size, transcendentals=pairs),
    )
    all_sums = to_all(own_sums, groups).reshape(blocks, BLK)
    row_grad, loss = run(
        rows_kernel,
        "anchor_rows",
        [jax.ShapeDtypeStruct((slots, width), f32), jax.ShapeDtypeStruct((8, BLK), f32)],
        [pltpu.VMEM((slots, BLK), f32)],
        plan,
        [embedded, info, acc, key_labels],
        keys,
        pl.CostEstimate(
            flops=2 * pairs * width, bytes_accessed=2 * keys.size, transcendentals=pairs
        ),
    )
    loss_parts = jnp.stack([jnp.sum(pixel_loss), loss[0, 0]])
    extra = jnp.broadcast_to(
        jnp.pad(loss_parts, (0, BLK - classes - 2))[None, :], (channels, BLK - classes)
    )
    class_part = jnp.concatenate([class_part, extra], axis=1)
    grad_projected, parts = run(
        keys_kernel,
        "anchor_keys",
        [
            jax.ShapeDtypeStruct((slots, width), f32),
            jax.ShapeDtypeStruct((channels, width + BLK), f32),
        ],
        [pltpu.VMEM((1, groups * slots), f32), pltpu.VMEM((slots, width), f32)],
        plan,
        [
            embedded,
            info,
            key_labels,
            key_ratio,
            key_floor,
            all_sums,
            row_grad,
            unit,
            length,
            picked,
            class_part,
        ],
        keys,
        pl.CostEstimate(
            flops=2 * pairs * width, bytes_accessed=2 * keys.size, transcendentals=pairs
        ),
    )

    share = channels // groups
    received = lax.all_to_all(
        parts.reshape(groups, share, width + BLK), "group", 0, 0, tiled=True
    )
    summed = to_all(jnp.sum(received, axis=0), groups).reshape(channels, width + BLK)
    grad_proj = summed[:, :width]
    grad_class = summed[:, width : width + classes]
    loss_sums = summed[0, width + classes : width + classes + 2]

    grad_picked = lax.dot_general(
        grad_projected,
        proj_weight.astype(f32),
        NT,
        precision=lax.Precision.HIGHEST,
        preferred_element_type=f32,
    )
    scattered = jnp.zeros((pixels, channels), f32).at[pix_ids].add(grad_picked)
    grad_features = (from_classes + scattered).astype(jnp.bfloat16)
    losses = loss_sums / jnp.stack([f32(groups * pixels), (valid * BLK).astype(f32)])
    return (grad_features, grad_proj, grad_class, losses)


def solution(mesh):
    return jax.shard_map(
        per_device,
        mesh=mesh,
        in_specs=(
            P(("dp", "group"), None),
            P(),
            P("dp", None),
            P("dp"),
            P(("dp", "group"), None),
            P("dp", None),
            P(("dp", "group")),
        ),
        out_specs=(P(("dp", "group"), None), P("dp", None), P("dp", None), P("dp")),
        check_vma=False,
    )
```

```python
import functools

import jax
import jax.numpy as jnp
from jax import lax
from jax.experimental import pallas as pl
from jax.experimental.pallas import tpu as pltpu
from jax.sharding import PartitionSpec as P

BLK = 128
SOON = 4
UNIT = 16
PARTS = BLK // UNIT
TILE = 512
ROOM = 40
INV_TEMP = 10.0
EXP_SCALE = INV_TEMP * 1.4426950408889634
NORM_EPS = 1e-06
VMEM_BYTES = 63 * 1024 * 1024

NN = (((1,), (0,)), ((), ()))
NT = (((1,), (1,)), ((), ()))
TN = (((0,), (0,)), ((), ()))
F32 = jnp.float32
BF16 = jnp.bfloat16


def dot_f32(left, right, dims=NN):
    return lax.dot_general(left, right, dims, preferred_element_type=F32)


def split_bf16(value, count):
    parts = []
    for _ in range(count):
        parts.append(value.astype(BF16))
        value = value - parts[-1].astype(F32)
    return parts


def blocks_before(blocks_ref, image):
    total = jnp.int32(0)
    for group in range(blocks_ref.shape[0]):
        total = total + jnp.where(group < image, blocks_ref[group], 0)
    return total


def each_block(blocks_ref, visit):
    place = jnp.int32(0)
    for image in range(blocks_ref.shape[0]):
        count = blocks_ref[image]
        for block in range(4):
            pl.when(block < count)(functools.partial(visit, image, block, place + block))
        place = place + count


def fold_lanes(value):
    total = value[:, :BLK]
    for start in range(BLK, value.shape[1], BLK):
        total = total + value[:, start : start + BLK]
    return total


def column_of(row, height=BLK):
    return jnp.broadcast_to(row, (height, row.shape[1])).T[:, 0:1]


def project(picked, proj):
    projected = dot_f32(picked, proj)
    length = jnp.sqrt(jnp.sum(projected * projected, axis=1, keepdims=True) + NORM_EPS)
    return projected / length, length


def pick_kernel(
    blocks_ref, pix_ref, features_hbm, proj_ref, picked_ref, emb_ref, send_ref, features, sems
):
    slots = pix_ref.shape[1]
    step = features.shape[0] // sems.shape[0]
    copies = [
        pltpu.make_async_copy(
            features_hbm.at[pl.ds(part * step, step)],
            features.at[pl.ds(part * step, step)],
            sems.at[part],
        )
        for part in range(sems.shape[0])
    ]
    for copy in copies:
        copy.start()
    pix = column_of(pix_ref[...].astype(F32)).astype(jnp.int32)
    lanes = lax.broadcasted_iota(jnp.int32, (slots, step), 1)
    total = jnp.zeros((slots, features.shape[1]), F32)
    for part, copy in enumerate(copies):
        onehot = jnp.where(lanes == pix - part * step, 1.0, 0.0).astype(BF16)
        copy.wait()
        total = total + dot_f32(onehot, features[part * step : (part + 1) * step, :])
    picked = total.astype(BF16)
    picked_ref[...] = picked
    unit, _ = project(picked, proj_ref[...])
    emb_ref[...] = unit.astype(BF16)
    odd = lax.rem(blocks_before(blocks_ref, lax.axis_index("group")), 2)
    for half in range(2):
        first = half + odd - 2 * half * odd
        for part in range(PARTS):
            for pair in range(slots // BLK // 2):
                start = pl.multiple_of((2 * pair + first) * BLK + part * UNIT, UNIT)
                send_ref[half * PARTS + part, pair * UNIT : (pair + 1) * UNIT, :] = emb_ref[
                    pl.ds(start, UNIT), :
                ]


def label_kernel(
    blocks_ref, labels_ref, picked_ref, proj_ref,
    key_label_ref, info_ref, lanes_ref, unit_ref, length_ref, wide,
):
    unit, length = project(picked_ref[...], proj_ref[...])
    unit_ref[...] = unit
    length_ref[...] = jnp.broadcast_to(length, length_ref.shape)
    me = lax.axis_index("group")
    slots = labels_ref.shape[1]
    key_label_ref[...] = jnp.full_like(key_label_ref, -1.0)

    def place_labels(image, block, place):
        span = pl.ds(pl.multiple_of(place * BLK, BLK), BLK)
        part = labels_ref[image : image + 1, block * BLK : (block + 1) * BLK]
        key_label_ref[:, span] = part.astype(F32)

    each_block(blocks_ref, place_labels)
    class_ids = lax.broadcasted_iota(jnp.int32, (BLK, BLK), 0).astype(F32)
    counts = jnp.zeros((BLK, BLK), F32)
    for start in range(0, key_label_ref.shape[1], BLK):
        counts = counts + jnp.where(class_ids == key_label_ref[:, start : start + BLK], 1.0, 0.0)
    histogram = jnp.sum(counts, axis=1, keepdims=True)
    images = lax.broadcasted_iota(jnp.int32, labels_ref.shape, 0)
    own = jnp.where(images == me, labels_ref[...].astype(F32), 0.0)
    own = jnp.sum(own, axis=0, keepdims=True)
    own_ids = lax.broadcasted_iota(jnp.int32, (BLK, slots), 0).astype(F32)
    same = jnp.sum(jnp.where(own_ids == own, histogram, 0.0), axis=0, keepdims=True)
    slot_ids = lax.broadcasted_iota(jnp.int32, (1, slots), 1)
    keep = jnp.where(slot_ids < blocks_ref[me] * BLK, 1.0, 0.0)
    wide[...] = jnp.zeros_like(wide)
    wide[0:1, :] = keep
    wide[1:2, :] = own
    wide[2:3, :] = keep * (same - 1.0)
    lanes_ref[...] = wide[0:8, :]
    info_ref[...] = wide[...].T


def pack_kernel(first_unit, blocks_ref, recv_ref, rep_hbm, packed, sems):
    half = lax.div(lax.axis_index("group"), PARTS)
    packed[...] = jnp.zeros_like(packed)
    units = packed.shape[0] // UNIT

    def one_image(image, place):
        odd = lax.rem(place, 2)
        first = half + odd - 2 * half * odd
        for pair in range(2):
            block = 2 * pair + first
            unit = lax.div(place + block, 2) - first_unit

            @pl.when((block < blocks_ref[image]) & (unit >= 0) & (unit < units))
            def _():
                packed[pl.ds(pl.multiple_of(unit * UNIT, UNIT), UNIT), :] = recv_ref[
                    image, pair * UNIT : (pair + 1) * UNIT, :
                ]

        return place + blocks_ref[image]

    lax.fori_loop(0, blocks_ref.shape[0], one_image, jnp.int32(0))
    copies = [
        pltpu.make_async_copy(packed, rep_hbm.at[device], sems.at[device])
        for device in range(rep_hbm.shape[0])
    ]
    for copy in copies:
        copy.start()
    for copy in copies:
        copy.wait()


def skip_kernel(blocks_ref, out_hbm):
    pass


def load_keys(valid, keys_hbm, more_hbm, keys, sems):
    units = keys_hbm.shape[1]
    more = more_hbm.shape[1]

    def copies_of(which, source, start, count, place):
        return [
            pltpu.make_async_copy(
                source.at[device, pl.ds(start, count)],
                keys.at[pl.ds(place, count), device // PARTS, device % PARTS],
                sems.at[which, device],
            )
            for device in range(2 * PARTS)
        ]

    first = copies_of(0, keys_hbm, 0, SOON, 0)
    later = copies_of(1, keys_hbm, SOON, units - SOON, SOON)
    last = copies_of(2, more_hbm, 0, more, units)
    for copy in first + later:
        copy.start()

    @pl.when(valid > ROOM)
    def _():
        for copy in last:
            copy.start()
        for copy in last:
            copy.wait()

    def wait_first():
        for copy in first:
            copy.wait()

    def wait_later():
        for copy in later:
            copy.wait()

    return wait_first, wait_later


def each_tile(valid, waits, visit):
    wait_first, wait_later = waits
    wait_first()
    for tile in range(ROOM * BLK // TILE):
        if tile == SOON // 2:
            wait_later()
        visit(tile)

    def later(tile, carry):
        visit(tile)
        return carry

    per_tile = TILE // BLK
    lax.fori_loop(ROOM // per_tile, lax.div(valid + per_tile - 1, per_tile), later, 0)


def key_tile_of(keys, tile):
    return keys[pl.ds(2 * tile, 2)].reshape(TILE, keys.shape[-1])


def lanes_of(tile):
    start = tile * TILE
    return pl.ds(start if isinstance(start, int) else pl.multiple_of(start, TILE), TILE)


def not_own(rows, first_place, tile):
    row_ids = lax.broadcasted_iota(jnp.int32, (rows, TILE), 0)
    lane_ids = lax.broadcasted_iota(jnp.int32, (rows, TILE), 1)
    return lane_ids - row_ids != first_place * BLK - tile * TILE


def sums_kernel(
    blocks_ref, lanes_ref, own_ref, keys_hbm, more_hbm, grad_ref, acc_ref, send_ref,
    keys, sems,
):
    valid = blocks_before(blocks_ref, blocks_ref.shape[0])
    waits = load_keys(valid, keys_hbm, more_hbm, keys, sems)
    first_place = blocks_before(blocks_ref, lax.axis_index("group"))
    acc_ref[...] = jnp.zeros_like(acc_ref)
    grad_ref[...] = jnp.zeros_like(grad_ref)
    own = own_ref[...]
    lane_ids = lax.broadcasted_iota(jnp.int32, (1, TILE), 1)

    def visit(tile):
        key_tile = key_tile_of(keys, tile)
        in_use = jnp.where(lane_ids < valid * BLK - tile * TILE, 1.0, 0.0)
        weights = jnp.exp(dot_f32(own, key_tile, NT) * INV_TEMP) * in_use
        weights = jnp.where(not_own(own.shape[0], first_place, tile), weights, 0.0)
        acc_ref[...] += fold_lanes(weights)
        grad_ref[...] += dot_f32(weights.astype(BF16), key_tile)

    each_tile(valid, waits, visit)
    for block in range(own.shape[0] // BLK):
        rows = slice(block * BLK, (block + 1) * BLK)
        total = jnp.sum(acc_ref[rows, :].T, axis=0, keepdims=True)
        pos_count = lanes_ref[2:3, rows]
        scale = pos_count / jnp.maximum(pos_count, 1.0) / total
        for device in range(send_ref.shape[0]):
            send_ref[device, block : block + 1, :] = scale


def rows_kernel(
    blocks_ref, own_ref, info_ref, acc_ref, sum_grad_ref, key_label_ref, keys_hbm, more_hbm,
    grad_ref, same_ref, keys, by_class, squares, sems,
):
    valid = blocks_before(blocks_ref, blocks_ref.shape[0])
    waits = load_keys(valid, keys_hbm, more_hbm, keys, sems)
    class_ids = lax.broadcasted_iota(jnp.int32, (BLK, TILE), 0).astype(F32)
    by_class[...] = jnp.zeros_like(by_class)
    squares[...] = jnp.zeros_like(squares)

    def visit(tile):
        key_tile = key_tile_of(keys, tile)
        member = class_ids == key_label_ref[:, lanes_of(tile)]
        member = jnp.where(member, 1.0, 0.0).astype(BF16)
        by_class[...] += dot_f32(member, key_tile)
        wide = key_tile.astype(F32)
        for part in split_bf16(wide * wide, 2):
            squares[...] += dot_f32(member, part)

    each_tile(valid, waits, visit)
    counts = jnp.zeros((BLK, BLK), F32)
    for start in range(0, key_label_ref.shape[1], BLK):
        counts = counts + jnp.where(
            class_ids[:, :BLK] == key_label_ref[:, start : start + BLK], 1.0, 0.0
        )
    others = jnp.sum(counts, axis=1, keepdims=True) - 1.0
    sums = by_class[...]
    pair_sum = jnp.sum(sums * sums - squares[...], axis=1, keepdims=True)
    pair_sum = jnp.where(others > 0.5, pair_sum / jnp.maximum(others, 1.0), 0.0)
    same_ref[...] = jnp.broadcast_to(
        INV_TEMP * jnp.sum(pair_sum, axis=0, keepdims=True), same_ref.shape
    )
    keep = info_ref[:, 0:1]
    pos_count = info_ref[:, 2:3]
    lane_ids = lax.broadcasted_iota(jnp.int32, info_ref.shape, 1).astype(F32)
    member = jnp.where(lane_ids == info_ref[:, 1:2], 1.0, 0.0).astype(BF16)
    others = sum(dot_f32(member, part) for part in split_bf16(sums, 3))
    others = others - own_ref[...].astype(F32)
    pos_floor = jnp.maximum(pos_count, 1.0)
    total = jnp.sum(acc_ref[...], axis=1, keepdims=True)
    row_scale = keep * (pos_count / pos_floor) / total
    grad_ref[...] = row_scale * sum_grad_ref[...] - (2.0 * keep / pos_floor) * others


def keys_kernel(
    blocks_ref, own_ref, info_ref, scales_ref, same_ref, row_grad_hbm, unit_hbm, length_hbm,
    picked_hbm, class_hbm, keys_hbm, more_hbm, grad_ref, out_ref,
    keys, scale, acc, row_grad, unit, length, picked, sems, end_sems,
):
    valid = blocks_before(blocks_ref, blocks_ref.shape[0])
    waits = load_keys(valid, keys_hbm, more_hbm, keys, sems)
    late = [
        pltpu.make_async_copy(source, target, end_sems.at[i])
        for i, (source, target) in enumerate(
            [
                (row_grad_hbm, row_grad),
                (unit_hbm, unit),
                (length_hbm, length),
                (picked_hbm, picked),
                (class_hbm, out_ref.at[:, pl.ds(unit.shape[1], BLK)]),
            ]
        )
    ]
    for copy in late:
        copy.start()
    first_place = blocks_before(blocks_ref, lax.axis_index("group"))
    scale[...] = jnp.zeros_like(scale)

    def place_scales(image, block, place):
        span = pl.ds(pl.multiple_of(place * BLK, BLK), BLK)
        scale[:, span] = scales_ref[image, block : block + 1, :]

    each_block(blocks_ref, place_scales)
    acc[...] = jnp.zeros_like(acc)
    own = own_ref[...]

    def visit(tile):
        key_tile = key_tile_of(keys, tile)
        weights = jnp.exp(dot_f32(own, key_tile, NT) * INV_TEMP) * scale[:, lanes_of(tile)]
        weights = jnp.where(not_own(own.shape[0], first_place, tile), weights, 0.0)
        acc[...] += dot_f32(weights.astype(BF16), key_tile)

    each_tile(valid, waits, visit)
    for copy in late:
        copy.wait()
    grad = row_grad[...] + info_ref[:, 0:1] * acc[...]
    radial = jnp.sum(unit[...] * grad, axis=1, keepdims=True)
    grad = (grad - unit[...] * radial) / length[:, 0:1]
    grad_ref[...] = grad
    width = grad.shape[1]
    out_ref[:, :width] = sum(dot_f32(picked[...], part) for part in split_bf16(grad, 3))
    scales = scale[...]
    logs = jnp.where(scales > 0.0, -jnp.log(jnp.where(scales > 0.0, scales, 1.0)), 0.0)
    loss = jnp.sum(logs, axis=1, keepdims=True) - same_ref[...]
    last = (out_ref.shape[0], 1)
    out_ref[:, width + BLK - 1 :] = jnp.broadcast_to(loss, last)


def features_kernel(pix_ref, grad_ref, proj_ref, logits_ref, class_ref, out_ref):
    rows = out_ref.shape[0]
    slots = pix_ref.shape[1]
    ids = pl.program_id(0) * rows + lax.broadcasted_iota(jnp.int32, (rows, slots), 0)
    onehot = jnp.where(ids == pix_ref[...], 1.0, 0.0).astype(BF16)
    proj = proj_ref[...]
    total = dot_f32(logits_ref[...], class_ref[...], NT)
    for part in split_bf16(grad_ref[...], 2):
        total = total + dot_f32(dot_f32(onehot, part).astype(BF16), proj, NT)
    out_ref[...] = total.astype(BF16)


def add_kernel(classes, recv_ref, rep_hbm, total_ref, sems):
    total = recv_ref[0]
    for device in range(1, recv_ref.shape[0]):
        total = total + recv_ref[device]
    high, middle, low = split_bf16(total, 3)
    rows = lax.broadcasted_iota(jnp.int32, total.shape, 0)
    is_loss = lax.broadcasted_iota(jnp.int32, total.shape, 1) >= total.shape[1] - BLK + classes
    parts = jnp.where(rows == 1, middle.astype(F32), low.astype(F32))
    value = jnp.where(is_loss & (rows > 0), parts, high.astype(F32))
    total_ref[...] = value.astype(BF16)
    copies = [
        pltpu.make_async_copy(total_ref, rep_hbm.at[device], sems.at[device])
        for device in range(rep_hbm.shape[0])
    ]
    for copy in copies:
        copy.start()
    for copy in copies:
        copy.wait()


def end_kernel(pixels, blocks_ref, summed_ref, proj_ref, class_ref, losses_ref):
    width = proj_ref.shape[1]
    classes = class_ref.shape[1]
    summed = summed_ref[...].astype(F32)
    proj_ref[...] = summed[:, :width]
    class_ref[...] = summed[:, width : width + classes]
    groups = blocks_ref.shape[0]
    anchors = (blocks_before(blocks_ref, groups) * (groups * BLK)).astype(F32)
    top = summed[:8, width:]
    rows = lax.broadcasted_iota(jnp.int32, top.shape, 0)
    lanes = lax.broadcasted_iota(jnp.int32, top.shape, 1)
    pixel_loss = jnp.sum(jnp.where((rows < 3) & (lanes == classes), top, 0.0))
    contrast = jnp.sum(jnp.where((rows < 3) & (lanes == BLK - 1), top, 0.0))
    losses_ref[0] = pixel_loss / pixels
    losses_ref[1] = contrast / anchors


SMEM = pl.BlockSpec(memory_space=pltpu.SMEM)
VMEM = pl.BlockSpec()
ANY = pl.BlockSpec(memory_space=pl.ANY)


def shape_of(shape, dtype=F32):
    return jax.ShapeDtypeStruct(shape, dtype)


def call(kernel, name, ins, outs, out_specs=None, scratch=(), flops=0, exps=0):
    size = sum(a.size * a.dtype.itemsize for a, _ in ins)
    size += sum(o.size * o.dtype.itemsize for o in outs)
    return pl.pallas_call(
        kernel,
        name=name,
        out_shape=outs,
        in_specs=[s for _, s in ins],
        out_specs=out_specs or [VMEM] * len(outs),
        scratch_shapes=list(scratch),
        compiler_params=pltpu.CompilerParams(vmem_limit_bytes=VMEM_BYTES),
        cost_estimate=pl.CostEstimate(flops=flops, bytes_accessed=size, transcendentals=exps),
    )(*[a for a, _ in ins])


def exchange(value):
    return lax.all_to_all(value, "group", 0, 0, tiled=True)


def per_device(
    features, proj_weight, class_weight, anchor_blocks, anchor_pix, anchor_label, pixel_label
):
    groups = lax.axis_size("group")
    slots = anchor_pix.shape[1]
    pixels, channels = features.shape
    classes = class_weight.shape[1]
    width = proj_weight.shape[1]
    per_image = slots // BLK
    blocks = groups * per_image
    share = channels // groups
    valid = jnp.sum(anchor_blocks)

    picked, emb, send = call(
        pick_kernel, "pick_anchors",
        [(anchor_blocks, SMEM), (anchor_pix, VMEM), (features, ANY), (proj_weight, VMEM)],
        [shape_of((slots, channels), BF16), shape_of((slots, width), BF16),
         shape_of((groups, slots // groups, width), BF16)],
        None, [pltpu.VMEM(features.shape, BF16), pltpu.SemaphoreType.DMA((4,))],
        flops=2 * slots * channels * (pixels + width),
    )
    recv = exchange(send)

    def packed(first_unit, units):
        (rep,) = call(
            functools.partial(pack_kernel, first_unit), "pack_keys",
            [(anchor_blocks, SMEM), (recv, VMEM)],
            [shape_of((groups, units * UNIT, width), BF16)], [ANY],
            [pltpu.VMEM((units * UNIT, width), BF16), pltpu.SemaphoreType.DMA((groups,))],
        )
        return rep

    units, more_units = ROOM // 2, (blocks - ROOM) // 2

    def second_exchange():
        return exchange(packed(units, more_units))

    def no_exchange():
        shape = shape_of((groups, more_units * UNIT, width), BF16)
        return call(skip_kernel, "skip_keys", [(anchor_blocks, SMEM)], [shape], [ANY])[0]

    rep = packed(0, units)
    keys = exchange(rep).reshape(groups, units, UNIT, width)
    more = lax.cond(valid > ROOM, second_exchange, no_exchange)
    more = more.reshape(groups, more_units, UNIT, width)

    labels, late_features, _ = lax.optimization_barrier((anchor_label, features, rep))
    key_label, info, lanes, unit, length = call(
        label_kernel, "anchor_labels",
        [(anchor_blocks, SMEM), (labels, VMEM), (picked, VMEM), (proj_weight, VMEM)],
        [shape_of((1, blocks * BLK)), shape_of((slots, BLK)), shape_of((8, slots)),
         shape_of((slots, width)), shape_of((slots, BLK))],
        None, [pltpu.VMEM((BLK, slots), F32)],
    )
    logits = jnp.dot(late_features, class_weight, preferred_element_type=F32)
    top_logit = jnp.max(logits, axis=1, keepdims=True)
    logsum_class = jnp.log(jnp.sum(jnp.exp(logits - top_logit), axis=1, keepdims=True)) + top_logit
    label_ids = jnp.arange(classes, dtype=jnp.int32)
    onehot = (pixel_label[:, None] == label_ids[None, :]).astype(F32)
    pixel_loss = jnp.sum(logsum_class[:, 0] - jnp.sum(onehot * logits, axis=1))
    grad_logits = (jnp.exp(logits - logsum_class) - onehot).astype(BF16)
    class_part = dot_f32(late_features, grad_logits, TN)
    tail = jnp.broadcast_to(pixel_loss, (channels, BLK - classes))
    class_part = jnp.concatenate([class_part, tail], axis=1)
    key_scratch = pltpu.VMEM((blocks // 2, 2, PARTS, UNIT, width), BF16)
    key_sems = [pltpu.SemaphoreType.DMA((3, groups))]
    pairs = slots * ROOM * BLK
    sum_grad, acc, sums = call(
        sums_kernel, "anchor_sums",
        [(anchor_blocks, SMEM), (lanes, VMEM), (emb, VMEM), (keys, ANY), (more, ANY)],
        [shape_of((slots, width)), shape_of((slots, BLK)), shape_of((groups, per_image, BLK))],
        None, [key_scratch] + key_sems, flops=4 * pairs * width, exps=pairs,
    )
    scales = exchange(sums)
    row_grad, same = call(
        rows_kernel, "anchor_rows",
        [(anchor_blocks, SMEM), (emb, VMEM), (info, VMEM), (acc, VMEM), (sum_grad, VMEM),
         (key_label, VMEM), (keys, ANY), (more, ANY)],
        [shape_of((slots, width)), shape_of((1, 1))],
        None,
        [key_scratch, pltpu.VMEM((BLK, width), F32), pltpu.VMEM((BLK, width), F32)] + key_sems,
        flops=6 * ROOM * BLK * BLK * width,
    )
    grad_projected, part = call(
        keys_kernel, "anchor_keys",
        [(anchor_blocks, SMEM), (emb, VMEM), (info, VMEM), (scales, VMEM), (same, VMEM),
         (row_grad, ANY), (unit, ANY), (length, ANY), (picked.T, ANY), (class_part, ANY),
         (keys, ANY), (more, ANY)],
        [shape_of((slots, width)), shape_of((channels, width + BLK))],
        None,
        [key_scratch, pltpu.VMEM((1, blocks * BLK), F32), pltpu.VMEM((slots, width), F32),
         pltpu.VMEM((slots, width), F32), pltpu.VMEM((slots, width), F32),
         pltpu.VMEM((slots, BLK), F32), pltpu.VMEM((channels, slots), BF16)]
        + key_sems + [pltpu.SemaphoreType.DMA((5,))],
        flops=4 * pairs * width, exps=pairs,
    )

    received = exchange(part.reshape(groups, share, width + BLK))
    tile = pixels // 4
    (grad_features,) = pl.pallas_call(
        features_kernel,
        name="feature_grads",
        grid=(pixels // tile,),
        out_shape=[shape_of((pixels, channels), BF16)],
        in_specs=[
            pl.BlockSpec((1, slots), lambda i: (0, 0)),
            pl.BlockSpec((slots, width), lambda i: (0, 0)),
            pl.BlockSpec((channels, width), lambda i: (0, 0)),
            pl.BlockSpec((tile, classes), lambda i: (i, 0)),
            pl.BlockSpec((channels, classes), lambda i: (0, 0)),
        ],
        out_specs=[pl.BlockSpec((tile, channels), lambda i: (i, 0))],
        compiler_params=pltpu.CompilerParams(vmem_limit_bytes=VMEM_BYTES),
        cost_estimate=pl.CostEstimate(
            flops=2 * pixels * (2 * slots * width + 2 * width * channels + classes * channels),
            bytes_accessed=4 * pixels * channels,
            transcendentals=0,
        ),
    )(anchor_pix, grad_projected, proj_weight, grad_logits, class_weight)
    (part_rep,) = call(
        functools.partial(add_kernel, classes), "add_shares", [(received, VMEM)],
        [shape_of(received.shape, BF16)], [ANY],
        [pltpu.VMEM(received.shape[1:], BF16), pltpu.SemaphoreType.DMA((groups,))],
    )
    summed = exchange(part_rep).reshape(channels, width + BLK)
    grad_proj, grad_class, losses = call(
        functools.partial(end_kernel, float(groups * pixels)), "outputs",
        [(anchor_blocks, SMEM), (summed, VMEM)],
        [shape_of((channels, width)), shape_of((channels, classes)), shape_of((2,))],
        [VMEM, VMEM, SMEM],
    )
    return (grad_features, grad_proj, grad_class, losses)


def solution(mesh):
    return jax.shard_map(
        per_device,
        mesh=mesh,
        in_specs=(
            P(("dp", "group"), None),
            P(),
            P("dp", None),
            P("dp"),
            P(("dp", "group"), None),
            P("dp", None),
            P(("dp", "group")),
        ),
        out_specs=(P(("dp", "group"), None), P("dp", None), P("dp", None), P("dp")),
        check_vma=False,
    )
```

```python
import functools

import jax
import jax.numpy as jnp
from jax import lax
from jax.experimental import pallas as pl
from jax.experimental.pallas import tpu as pltpu
from jax.sharding import PartitionSpec as P

BLK = 128
SOON = (0, 2, 8)
UNIT = 16
PARTS = BLK // UNIT
TILE = 512
ROOM = 40
INV_TEMP = 10.0
EXP_SCALE = INV_TEMP * 1.4426950408889634
NORM_EPS = 1e-06
VMEM_BYTES = 63 * 1024 * 1024
MID_BYTES = 40 * 1024 * 1024
LABEL_BYTES = 63 * 1024 * 1024
SMALL_BYTES = 16 * 1024 * 1024

NN = (((1,), (0,)), ((), ()))
NT = (((1,), (1,)), ((), ()))
TN = (((0,), (0,)), ((), ()))
F32 = jnp.float32
BF16 = jnp.bfloat16


def dot_f32(left, right, dims=NN):
    return lax.dot_general(left, right, dims, preferred_element_type=F32)


def split_bf16(value, count):
    parts = []
    for _ in range(count):
        parts.append(value.astype(BF16))
        value = value - parts[-1].astype(F32)
    return parts


def blocks_before(blocks_ref, image):
    total = jnp.int32(0)
    for group in range(blocks_ref.shape[0]):
        total = total + jnp.where(group < image, blocks_ref[group], 0)
    return total


def each_block(blocks_ref, visit):
    place = jnp.int32(0)
    for image in range(blocks_ref.shape[0]):
        count = blocks_ref[image]
        for block in range(4):
            pl.when(block < count)(functools.partial(visit, image, block, place + block))
        place = place + count


def fold_lanes(value):
    total = value[:, :BLK]
    for start in range(BLK, value.shape[1], BLK):
        total = total + value[:, start : start + BLK]
    return total


def column_of(row, height=BLK):
    return jnp.broadcast_to(row, (height, row.shape[1])).T[:, 0:1]


def project(picked, proj):
    projected = dot_f32(picked, proj)
    length = jnp.sqrt(jnp.sum(projected * projected, axis=1, keepdims=True) + NORM_EPS)
    return projected / length, length


def pick(pix_ref, features_hbm, features, sems, beside):
    slots = pix_ref.shape[1]
    step = features.shape[0] // sems.shape[0]
    copies = [
        pltpu.make_async_copy(
            features_hbm.at[pl.ds(part * step, step)],
            features.at[pl.ds(part * step, step)],
            sems.at[part],
        )
        for part in range(sems.shape[0])
    ]
    for copy in copies:
        copy.start()
    beside()
    pix = column_of(pix_ref[...].astype(F32)).astype(jnp.int32)
    lanes = lax.broadcasted_iota(jnp.int32, (slots, step), 1)
    total = jnp.zeros((slots, features.shape[1]), F32)
    for part, copy in enumerate(copies):
        onehot = jnp.where(lanes == pix - part * step, 1.0, 0.0).astype(BF16)
        copy.wait()
        total = total + dot_f32(onehot, features[part * step : (part + 1) * step, :])
    return total


def pick_kernel(
    blocks_ref, pix_ref, features_hbm, proj_ref, emb_ref, send_ref, features, sems
):
    slots = pix_ref.shape[1]
    picked = pick(pix_ref, features_hbm, features, sems, lambda: None).astype(BF16)
    unit, _ = project(picked, proj_ref[...])
    emb_ref[...] = unit.astype(BF16)
    odd = lax.rem(blocks_before(blocks_ref, lax.axis_index("group")), 2)
    for half in range(2):
        first = half + odd - 2 * half * odd
        for part in range(PARTS):
            for pair in range(slots // BLK // 2):
                start = pl.multiple_of((2 * pair + first) * BLK + part * UNIT, UNIT)
                send_ref[half * PARTS + part, pair * UNIT : (pair + 1) * UNIT, :] = emb_ref[
                    pl.ds(start, UNIT), :
                ]


def label_kernel(
    blocks_ref, labels_ref, pix_ref, features_hbm, proj_ref,
    key_label_ref, info_ref, lanes_ref, unit_ref, scale_ref, picked_ref, wide, features, sems,
):
    def labels():
        label_terms(blocks_ref, labels_ref, key_label_ref, info_ref, lanes_ref, wide)

    picked = pick(pix_ref, features_hbm, features, sems, labels)
    picked_ref[...] = picked.T.astype(BF16)
    unit, length = project(picked.astype(BF16), proj_ref[...])
    unit_ref[...] = unit
    scale_ref[...] = jnp.broadcast_to(info_ref[:, 0:1] / length, scale_ref.shape)


def label_terms(blocks_ref, labels_ref, key_label_ref, info_ref, lanes_ref, wide):
    me = lax.axis_index("group")
    slots = labels_ref.shape[1]
    key_label_ref[...] = jnp.full_like(key_label_ref, -1.0)

    def place_labels(image, block, place):
        span = pl.ds(pl.multiple_of(place * BLK, BLK), BLK)
        part = labels_ref[image : image + 1, block * BLK : (block + 1) * BLK]
        key_label_ref[:, span] = part.astype(F32)

    each_block(blocks_ref, place_labels)
    class_ids = lax.broadcasted_iota(jnp.int32, (BLK, BLK), 0).astype(F32)
    counts = jnp.zeros((BLK, BLK), F32)
    for start in range(0, key_label_ref.shape[1], BLK):
        counts = counts + jnp.where(class_ids == key_label_ref[:, start : start + BLK], 1.0, 0.0)
    histogram = jnp.sum(counts, axis=1, keepdims=True)
    images = lax.broadcasted_iota(jnp.int32, labels_ref.shape, 0)
    own = jnp.where(images == me, labels_ref[...].astype(F32), 0.0)
    own = jnp.sum(own, axis=0, keepdims=True)
    own_ids = lax.broadcasted_iota(jnp.int32, (BLK, slots), 0).astype(F32)
    same = jnp.sum(jnp.where(own_ids == own, histogram, 0.0), axis=0, keepdims=True)
    slot_ids = lax.broadcasted_iota(jnp.int32, (1, slots), 1)
    keep = jnp.where(slot_ids < blocks_ref[me] * BLK, 1.0, 0.0)
    wide[...] = jnp.zeros_like(wide)
    wide[0:1, :] = keep
    wide[1:2, :] = own
    wide[2:3, :] = keep * (same - 1.0)
    lanes_ref[...] = wide[0:8, :]
    info_ref[...] = wide[...].T


def pack_kernel(first_unit, blocks_ref, recv_ref, rep_hbm, packed, sems):
    half = lax.div(lax.axis_index("group"), PARTS)
    packed[...] = jnp.zeros_like(packed)
    units = packed.shape[0] // UNIT

    def one_image(image, place):
        odd = lax.rem(place, 2)
        first = half + odd - 2 * half * odd
        for pair in range(2):
            block = 2 * pair + first
            unit = lax.div(place + block, 2) - first_unit

            @pl.when((block < blocks_ref[image]) & (unit >= 0) & (unit < units))
            def _():
                packed[pl.ds(pl.multiple_of(unit * UNIT, UNIT), UNIT), :] = recv_ref[
                    image, pair * UNIT : (pair + 1) * UNIT, :
                ]

        return place + blocks_ref[image]

    lax.fori_loop(0, blocks_ref.shape[0], one_image, jnp.int32(0))
    copies = [
        pltpu.make_async_copy(packed, rep_hbm.at[device], sems.at[device])
        for device in range(rep_hbm.shape[0])
    ]
    for copy in copies:
        copy.start()
    for copy in copies:
        copy.wait()


def skip_kernel(blocks_ref, out_hbm):
    pass


def load_keys(valid, keys_hbm, more_hbm, keys, sems):
    units = keys_hbm.shape[1]
    more = more_hbm.shape[1]

    def copies_of(which, source, start, count, place):
        return [
            pltpu.make_async_copy(
                source.at[device, pl.ds(start, count)],
                keys.at[pl.ds(place, count), device // PARTS, device % PARTS],
                sems.at[which, device],
            )
            for device in range(2 * PARTS)
        ]

    starts = [start for start in SOON if start < units]
    waits = {}
    for which, (start, end) in enumerate(zip(starts, starts[1:] + [units])):
        copies = copies_of(which, keys_hbm, start, end - start, start)
        for copy in copies:
            copy.start()
        waits[start // 2] = copies
    last = copies_of(len(SOON), more_hbm, 0, more, units)

    @pl.when(valid > ROOM)
    def _():
        for copy in last:
            copy.start()
        for copy in last:
            copy.wait()

    return waits


def each_tile(valid, waits, visit):
    for tile in range(ROOM * BLK // TILE):
        for copy in waits.get(tile, ()):
            copy.wait()
        if (tile + 1) * TILE < ROOM * BLK:
            visit(tile)
        else:
            pl.when(valid > tile * (TILE // BLK))(functools.partial(visit, tile))

    def later(tile, carry):
        visit(tile)
        return carry

    per_tile = TILE // BLK
    lax.fori_loop(ROOM // per_tile, lax.div(valid + per_tile - 1, per_tile), later, 0)


def key_tile_of(keys, tile):
    return keys[pl.ds(2 * tile, 2)].reshape(TILE, keys.shape[-1])


def lanes_of(tile):
    start = tile * TILE
    return pl.ds(start if isinstance(start, int) else pl.multiple_of(start, TILE), TILE)


def not_own(rows, first_place, tile):
    row_ids = lax.broadcasted_iota(jnp.int32, (rows, TILE), 0)
    lane_ids = lax.broadcasted_iota(jnp.int32, (rows, TILE), 1)
    return lane_ids - row_ids != first_place * BLK - tile * TILE


def sums_kernel(
    blocks_ref, lanes_ref, own_ref, keys_hbm, more_hbm, grad_ref, acc_ref, send_ref,
    keys, sems,
):
    valid = blocks_before(blocks_ref, blocks_ref.shape[0])
    waits = load_keys(valid, keys_hbm, more_hbm, keys, sems)
    first_place = blocks_before(blocks_ref, lax.axis_index("group"))
    acc_ref[...] = jnp.zeros_like(acc_ref)
    grad_ref[...] = jnp.zeros_like(grad_ref)
    own = own_ref[...]
    lane_ids = lax.broadcasted_iota(jnp.int32, (1, TILE), 1)

    def visit(tile):
        key_tile = key_tile_of(keys, tile)
        in_use = jnp.where(lane_ids < valid * BLK - tile * TILE, 1.0, 0.0)
        weights = jnp.exp(dot_f32(own, key_tile, NT) * INV_TEMP) * in_use
        weights = jnp.where(not_own(own.shape[0], first_place, tile), weights, 0.0)
        acc_ref[...] += fold_lanes(weights)
        grad_ref[...] += dot_f32(weights.astype(BF16), key_tile)

    each_tile(valid, waits, visit)
    for block in range(own.shape[0] // BLK):
        rows = slice(block * BLK, (block + 1) * BLK)
        total = jnp.sum(acc_ref[rows, :].T, axis=0, keepdims=True)
        pos_count = lanes_ref[2:3, rows]
        scale = pos_count / jnp.maximum(pos_count, 1.0) / total
        for device in range(send_ref.shape[0]):
            send_ref[device, block : block + 1, :] = scale


def rows_kernel(
    blocks_ref, own_ref, info_ref, acc_ref, sum_grad_ref, key_label_ref, keys_hbm, more_hbm,
    grad_ref, loss_ref, keys, by_class, sems,
):
    valid = blocks_before(blocks_ref, blocks_ref.shape[0])
    waits = load_keys(valid, keys_hbm, more_hbm, keys, sems)
    class_ids = lax.broadcasted_iota(jnp.int32, (BLK, TILE), 0).astype(F32)
    by_class[...] = jnp.zeros_like(by_class)

    def visit(tile):
        member = class_ids == key_label_ref[:, lanes_of(tile)]
        member = jnp.where(member, 1.0, 0.0).astype(BF16)
        by_class[...] += dot_f32(member, key_tile_of(keys, tile))

    each_tile(valid, waits, visit)
    keep = info_ref[:, 0:1]
    pos_count = info_ref[:, 2:3]
    lane_ids = lax.broadcasted_iota(jnp.int32, info_ref.shape, 1).astype(F32)
    member = jnp.where(lane_ids == info_ref[:, 1:2], 1.0, 0.0).astype(BF16)
    own = own_ref[...].astype(F32)
    others = sum(dot_f32(member, part) for part in split_bf16(by_class[...], 3)) - own
    pos_floor = jnp.maximum(pos_count, 1.0)
    total = jnp.sum(acc_ref[...], axis=1, keepdims=True)
    row_scale = keep * (pos_count / pos_floor) / total
    grad_ref[...] = row_scale * sum_grad_ref[...] - (2.0 * keep / pos_floor) * others
    same_sum = INV_TEMP * jnp.sum(own * others, axis=1, keepdims=True)
    loss = keep * (pos_count * jnp.log(total) - same_sum) / pos_floor
    loss = jnp.sum(loss, axis=0, keepdims=True)
    loss_ref[...] = jnp.broadcast_to(loss, loss_ref.shape)


def keys_kernel(
    blocks_ref, own_ref, scales_ref, loss_ref, row_grad_hbm, unit_hbm, length_hbm, picked_hbm, class_hbm,
    keys_hbm, more_hbm, grad_ref, out_ref,
    keys, scale, acc, row_grad, unit, length, picked, sems, end_sems,
):
    valid = blocks_before(blocks_ref, blocks_ref.shape[0])
    waits = load_keys(valid, keys_hbm, more_hbm, keys, sems)
    late = [
        pltpu.make_async_copy(source, target, end_sems.at[i])
        for i, (source, target) in enumerate(
            [
                (row_grad_hbm, row_grad),
                (unit_hbm, unit),
                (length_hbm, length),
                (picked_hbm, picked),
                (class_hbm, out_ref.at[:, pl.ds(unit.shape[1], BLK)]),
            ]
        )
    ]
    for copy in late:
        copy.start()
    first_place = blocks_before(blocks_ref, lax.axis_index("group"))
    scale[...] = jnp.zeros_like(scale)
    place = jnp.int32(0)
    for image in range(blocks_ref.shape[0]):
        for block in range(scales_ref.shape[1]):
            scale[pl.ds(place + block, 1), :] = scales_ref[image, block : block + 1, :]
        place = place + blocks_ref[image]
    acc[...] = jnp.zeros_like(acc)
    own = own_ref[...]

    def visit(tile):
        key_tile = key_tile_of(keys, tile)
        per_tile = TILE // BLK
        key_scale = jnp.concatenate(
            [scale[pl.ds(tile * per_tile + i, 1), :] for i in range(per_tile)], axis=1
        )
        weights = jnp.exp(dot_f32(own, key_tile, NT) * INV_TEMP) * key_scale
        weights = jnp.where(not_own(own.shape[0], first_place, tile), weights, 0.0)
        acc[...] += dot_f32(weights.astype(BF16), key_tile)

    each_tile(valid, waits, visit)
    for copy in late:
        copy.wait()
    grad = row_grad[...] + acc[...]
    radial = jnp.sum(unit[...] * grad, axis=1, keepdims=True)
    grad = (grad - unit[...] * radial) * length[:, 0:1]
    grad_ref[...] = grad
    width = grad.shape[1]
    out_ref[:, :width] = sum(dot_f32(picked[...], part) for part in split_bf16(grad, 3))
    last = (out_ref.shape[0], 1)
    out_ref[:, width + BLK - 1 :] = jnp.broadcast_to(loss_ref[0:1, 0:1], last)


def features_kernel(pix_ref, grad_ref, proj_ref, logits_ref, class_ref, out_ref):
    rows = out_ref.shape[0]
    slots = pix_ref.shape[1]
    ids = pl.program_id(0) * rows + lax.broadcasted_iota(jnp.int32, (rows, slots), 0)
    onehot = jnp.where(ids == pix_ref[...], 1.0, 0.0).astype(BF16)
    proj = proj_ref[...]
    total = dot_f32(logits_ref[...], class_ref[...], NT)
    for part in split_bf16(grad_ref[...], 2):
        total = total + dot_f32(dot_f32(onehot, part).astype(BF16), proj, NT)
    out_ref[...] = total.astype(BF16)


def add_kernel(classes, recv_ref, rep_hbm, total_ref, sems):
    total = recv_ref[0]
    for device in range(1, recv_ref.shape[0]):
        total = total + recv_ref[device]
    high, middle, low = split_bf16(total, 3)
    rows = lax.broadcasted_iota(jnp.int32, total.shape, 0)
    is_loss = lax.broadcasted_iota(jnp.int32, total.shape, 1) >= total.shape[1] - BLK + classes
    parts = jnp.where(rows == 1, middle.astype(F32), low.astype(F32))
    value = jnp.where(is_loss & (rows > 0), parts, high.astype(F32))
    total_ref[...] = value.astype(BF16)
    copies = [
        pltpu.make_async_copy(total_ref, rep_hbm.at[device], sems.at[device])
        for device in range(rep_hbm.shape[0])
    ]
    for copy in copies:
        copy.start()
    for copy in copies:
        copy.wait()


def end_kernel(pixels, blocks_ref, summed_ref, proj_ref, class_ref, losses_ref):
    width = proj_ref.shape[1]
    classes = class_ref.shape[1]
    summed = summed_ref[...].astype(F32)
    proj_ref[...] = summed[:, :width]
    class_ref[...] = summed[:, width : width + classes]
    groups = blocks_ref.shape[0]
    anchors = (blocks_before(blocks_ref, groups) * BLK).astype(F32)
    top = summed[:8, width:]
    rows = lax.broadcasted_iota(jnp.int32, top.shape, 0)
    lanes = lax.broadcasted_iota(jnp.int32, top.shape, 1)
    pixel_loss = jnp.sum(jnp.where((rows < 3) & (lanes == classes), top, 0.0))
    contrast = jnp.sum(jnp.where((rows < 3) & (lanes == BLK - 1), top, 0.0))
    losses_ref[0] = pixel_loss / pixels
    losses_ref[1] = contrast / anchors


SMEM = pl.BlockSpec(memory_space=pltpu.SMEM)
VMEM = pl.BlockSpec()
ANY = pl.BlockSpec(memory_space=pl.ANY)


def shape_of(shape, dtype=F32):
    return jax.ShapeDtypeStruct(shape, dtype)


def call(kernel, name, ins, outs, out_specs=None, scratch=(), flops=0, exps=0, vmem=VMEM_BYTES):
    size = sum(a.size * a.dtype.itemsize for a, _ in ins)
    size += sum(o.size * o.dtype.itemsize for o in outs)
    return pl.pallas_call(
        kernel,
        name=name,
        out_shape=outs,
        in_specs=[s for _, s in ins],
        out_specs=out_specs or [VMEM] * len(outs),
        scratch_shapes=list(scratch),
        compiler_params=pltpu.CompilerParams(vmem_limit_bytes=vmem),
        cost_estimate=pl.CostEstimate(flops=flops, bytes_accessed=size, transcendentals=exps),
    )(*[a for a, _ in ins])


def exchange(value):
    return lax.all_to_all(value, "group", 0, 0, tiled=True)


def per_device(
    features, proj_weight, class_weight, anchor_blocks, anchor_pix, anchor_label, pixel_label
):
    groups = lax.axis_size("group")
    slots = anchor_pix.shape[1]
    pixels, channels = features.shape
    classes = class_weight.shape[1]
    width = proj_weight.shape[1]
    per_image = slots // BLK
    blocks = groups * per_image
    share = channels // groups
    valid = jnp.sum(anchor_blocks)

    emb, send = call(
        pick_kernel, "pick_anchors",
        [(anchor_blocks, SMEM), (anchor_pix, VMEM), (features, ANY), (proj_weight, VMEM)],
        [shape_of((slots, width), BF16), shape_of((groups, slots // groups, width), BF16)],
        None, [pltpu.VMEM(features.shape, BF16), pltpu.SemaphoreType.DMA((4,))],
        flops=2 * slots * channels * (pixels + width),
    )
    recv = exchange(send)

    def packed(first_unit, units):
        (rep,) = call(
            functools.partial(pack_kernel, first_unit), "pack_keys",
            [(anchor_blocks, SMEM), (recv, VMEM)],
            [shape_of((groups, units * UNIT, width), BF16)], [ANY],
            [pltpu.VMEM((units * UNIT, width), BF16), pltpu.SemaphoreType.DMA((groups,))],
        )
        return rep

    units, more_units = ROOM // 2, (blocks - ROOM) // 2

    def second_exchange():
        return exchange(packed(units, more_units))

    def no_exchange():
        shape = shape_of((groups, more_units * UNIT, width), BF16)
        return call(skip_kernel, "skip_keys", [(anchor_blocks, SMEM)], [shape], [ANY])[0]

    rep = packed(0, units)
    keys = exchange(rep).reshape(groups, units, UNIT, width)
    more = lax.cond(valid > ROOM, second_exchange, no_exchange)
    more = more.reshape(groups, more_units, UNIT, width)

    labels, late_features, _ = lax.optimization_barrier((anchor_label, features, rep))
    key_label, info, lanes, unit, scale, picked_t = call(
        label_kernel, "anchor_labels",
        [(anchor_blocks, SMEM), (labels, VMEM), (anchor_pix, VMEM), (late_features, ANY),
         (proj_weight, VMEM)],
        [shape_of((1, blocks * BLK)), shape_of((slots, BLK)), shape_of((8, slots)),
         shape_of((slots, width)), shape_of((slots, BLK)), shape_of((channels, slots), BF16)],
        None,
        [pltpu.VMEM((BLK, slots), F32), pltpu.VMEM(features.shape, BF16),
         pltpu.SemaphoreType.DMA((4,))],
        vmem=LABEL_BYTES,
    )
    logits = jnp.dot(late_features, class_weight, preferred_element_type=F32)
    top_logit = jnp.max(logits, axis=1, keepdims=True)
    logsum_class = jnp.log(jnp.sum(jnp.exp(logits - top_logit), axis=1, keepdims=True)) + top_logit
    label_ids = jnp.arange(classes, dtype=jnp.int32)
    onehot = (pixel_label[:, None] == label_ids[None, :]).astype(F32)
    pixel_loss = jnp.sum(logsum_class[:, 0] - jnp.sum(onehot * logits, axis=1))
    grad_logits = (jnp.exp(logits - logsum_class) - onehot).astype(BF16)
    class_part = dot_f32(late_features, grad_logits, TN)
    tail = jnp.broadcast_to(pixel_loss, (channels, BLK - classes))
    class_part = jnp.concatenate([class_part, tail], axis=1)
    key_scratch = pltpu.VMEM((blocks // 2, 2, PARTS, UNIT, width), BF16)
    key_sems = [pltpu.SemaphoreType.DMA((len(SOON) + 1, groups))]
    pairs = slots * ROOM * BLK
    sum_grad, acc, sums = call(
        sums_kernel, "anchor_sums",
        [(anchor_blocks, SMEM), (lanes, VMEM), (emb, VMEM), (keys, ANY), (more, ANY)],
        [shape_of((slots, width)), shape_of((slots, BLK)), shape_of((groups, per_image, BLK))],
        None, [key_scratch] + key_sems, flops=4 * pairs * width, exps=pairs, vmem=MID_BYTES,
    )
    scales = exchange(sums)
    row_grad, loss = call(
        rows_kernel, "anchor_rows",
        [(anchor_blocks, SMEM), (emb, VMEM), (info, VMEM), (acc, VMEM), (sum_grad, VMEM),
         (key_label, VMEM), (keys, ANY), (more, ANY)],
        [shape_of((slots, width)), shape_of((8, BLK))],
        None, [key_scratch, pltpu.VMEM((BLK, width), F32)] + key_sems,
        flops=2 * ROOM * BLK * BLK * width, vmem=MID_BYTES,
    )
    grad_projected, part = call(
        keys_kernel, "anchor_keys",
        [(anchor_blocks, SMEM), (emb, VMEM), (scales, VMEM), (loss, VMEM), (row_grad, ANY),
         (unit, ANY), (scale, ANY), (picked_t, ANY), (class_part, ANY), (keys, ANY), (more, ANY)],
        [shape_of((slots, width)), shape_of((channels, width + BLK))],
        None,
        [key_scratch, pltpu.VMEM((blocks + 8, BLK), F32), pltpu.VMEM((slots, width), F32),
         pltpu.VMEM((slots, width), F32), pltpu.VMEM((slots, width), F32),
         pltpu.VMEM((slots, BLK), F32), pltpu.VMEM((channels, slots), BF16)]
        + key_sems + [pltpu.SemaphoreType.DMA((5,))],
        flops=4 * pairs * width, exps=pairs, vmem=MID_BYTES,
    )

    received = exchange(part.reshape(groups, share, width + BLK))
    tile = pixels // 4
    (grad_features,) = pl.pallas_call(
        features_kernel,
        name="feature_grads",
        grid=(pixels // tile,),
        out_shape=[shape_of((pixels, channels), BF16)],
        in_specs=[
            pl.BlockSpec((1, slots), lambda i: (0, 0)),
            pl.BlockSpec((slots, width), lambda i: (0, 0)),
            pl.BlockSpec((channels, width), lambda i: (0, 0)),
            pl.BlockSpec((tile, classes), lambda i: (i, 0)),
            pl.BlockSpec((channels, classes), lambda i: (0, 0)),
        ],
        out_specs=[pl.BlockSpec((tile, channels), lambda i: (i, 0))],
        compiler_params=pltpu.CompilerParams(vmem_limit_bytes=VMEM_BYTES),
        cost_estimate=pl.CostEstimate(
            flops=2 * pixels * (2 * slots * width + 2 * width * channels + classes * channels),
            bytes_accessed=4 * pixels * channels,
            transcendentals=0,
        ),
    )(anchor_pix, grad_projected, proj_weight, grad_logits, class_weight)
    (part_rep,) = call(
        functools.partial(add_kernel, classes), "add_shares", [(received, VMEM)],
        [shape_of(received.shape, BF16)], [ANY],
        [pltpu.VMEM(received.shape[1:], BF16), pltpu.SemaphoreType.DMA((groups,))],
        vmem=SMALL_BYTES,
    )
    summed = exchange(part_rep).reshape(channels, width + BLK)
    grad_proj, grad_class, losses = call(
        functools.partial(end_kernel, float(groups * pixels)), "outputs",
        [(anchor_blocks, SMEM), (summed, VMEM)],
        [shape_of((channels, width)), shape_of((channels, classes)), shape_of((2,))],
        [VMEM, VMEM, SMEM], vmem=SMALL_BYTES,
    )
    return (grad_features, grad_proj, grad_class, losses)


def solution(mesh):
    return jax.shard_map(
        per_device,
        mesh=mesh,
        in_specs=(
            P(("dp", "group"), None),
            P(),
            P("dp", None),
            P("dp"),
            P(("dp", "group"), None),
            P("dp", None),
            P(("dp", "group")),
        ),
        out_specs=(P(("dp", "group"), None), P("dp", None), P("dp", None), P("dp")),
        check_vma=False,
    )
```

```python
import functools

import jax
import jax.numpy as jnp
from jax import lax
from jax.experimental import pallas as pl
from jax.experimental.pallas import tpu as pltpu
from jax.sharding import PartitionSpec as P

BLK = 128
SOON = (0, 2, 8)
UNIT = 16
PARTS = BLK // UNIT
TILE = 512
ROOM = 40
INV_TEMP = 10.0
EXP_SCALE = INV_TEMP * 1.4426950408889634
NORM_EPS = 1e-06
VMEM_BYTES = 63 * 1024 * 1024
MID_BYTES = 40 * 1024 * 1024
LABEL_BYTES = 63 * 1024 * 1024
SMALL_BYTES = 16 * 1024 * 1024

NN = (((1,), (0,)), ((), ()))
NT = (((1,), (1,)), ((), ()))
TN = (((0,), (0,)), ((), ()))
F32 = jnp.float32
BF16 = jnp.bfloat16


def dot_f32(left, right, dims=NN):
    return lax.dot_general(left, right, dims, preferred_element_type=F32)


def split_bf16(value, count):
    parts = []
    for _ in range(count):
        parts.append(value.astype(BF16))
        value = value - parts[-1].astype(F32)
    return parts


def blocks_before(blocks_ref, image):
    total = jnp.int32(0)
    for group in range(blocks_ref.shape[0]):
        total = total + jnp.where(group < image, blocks_ref[group], 0)
    return total


def each_block(blocks_ref, visit):
    place = jnp.int32(0)
    for image in range(blocks_ref.shape[0]):
        count = blocks_ref[image]
        for block in range(4):
            pl.when(block < count)(functools.partial(visit, image, block, place + block))
        place = place + count


def fold_lanes(value):
    total = value[:, :BLK]
    for start in range(BLK, value.shape[1], BLK):
        total = total + value[:, start : start + BLK]
    return total


def column_of(row, height=BLK):
    return jnp.broadcast_to(row, (height, row.shape[1])).T[:, 0:1]


def project(picked, proj):
    projected = dot_f32(picked, proj)
    length = jnp.sqrt(jnp.sum(projected * projected, axis=1, keepdims=True) + NORM_EPS)
    return projected / length, length


def pick(pix_ref, features_hbm, features, sems, beside):
    slots = pix_ref.shape[1]
    step = features.shape[0] // sems.shape[0]
    copies = [
        pltpu.make_async_copy(
            features_hbm.at[pl.ds(part * step, step)],
            features.at[pl.ds(part * step, step)],
            sems.at[part],
        )
        for part in range(sems.shape[0])
    ]
    for copy in copies:
        copy.start()
    beside()
    pix = column_of(pix_ref[...].astype(F32)).astype(jnp.int32)
    lanes = lax.broadcasted_iota(jnp.int32, (slots, step), 1)
    total = jnp.zeros((slots, features.shape[1]), F32)
    for part, copy in enumerate(copies):
        onehot = jnp.where(lanes == pix - part * step, 1.0, 0.0).astype(BF16)
        copy.wait()
        total = total + dot_f32(onehot, features[part * step : (part + 1) * step, :])
    return total


def pick_kernel(
    blocks_ref, pix_ref, features_hbm, proj_ref, emb_ref, send_ref, features, sems
):
    slots = pix_ref.shape[1]
    picked = pick(pix_ref, features_hbm, features, sems, lambda: None).astype(BF16)
    unit, _ = project(picked, proj_ref[...])
    emb_ref[...] = unit.astype(BF16)
    odd = lax.rem(blocks_before(blocks_ref, lax.axis_index("group")), 2)
    for half in range(2):
        first = half + odd - 2 * half * odd
        for part in range(PARTS):
            for pair in range(slots // BLK // 2):
                start = pl.multiple_of((2 * pair + first) * BLK + part * UNIT, UNIT)
                send_ref[half * PARTS + part, pair * UNIT : (pair + 1) * UNIT, :] = emb_ref[
                    pl.ds(start, UNIT), :
                ]


def label_kernel(
    blocks_ref, labels_ref, pix_ref, features_hbm, proj_ref,
    key_label_ref, info_ref, lanes_ref, unit_ref, scale_ref, picked_ref, wide, features, sems,
):
    def labels():
        label_terms(blocks_ref, labels_ref, key_label_ref, info_ref, lanes_ref, wide)

    picked = pick(pix_ref, features_hbm, features, sems, labels)
    picked_ref[...] = picked.T.astype(BF16)
    unit, length = project(picked.astype(BF16), proj_ref[...])
    unit_ref[...] = unit
    scale_ref[...] = jnp.broadcast_to(info_ref[:, 0:1] / length, scale_ref.shape)


def label_terms(blocks_ref, labels_ref, key_label_ref, info_ref, lanes_ref, wide):
    me = lax.axis_index("group")
    slots = labels_ref.shape[1]
    key_label_ref[...] = jnp.full_like(key_label_ref, -1.0)

    def place_labels(image, block, place):
        span = pl.ds(pl.multiple_of(place * BLK, BLK), BLK)
        part = labels_ref[image : image + 1, block * BLK : (block + 1) * BLK]
        key_label_ref[:, span] = part.astype(F32)

    each_block(blocks_ref, place_labels)
    class_ids = lax.broadcasted_iota(jnp.int32, (BLK, BLK), 0).astype(F32)
    counts = jnp.zeros((BLK, BLK), F32)
    for start in range(0, key_label_ref.shape[1], BLK):
        counts = counts + jnp.where(class_ids == key_label_ref[:, start : start + BLK], 1.0, 0.0)
    histogram = jnp.sum(counts, axis=1, keepdims=True)
    images = lax.broadcasted_iota(jnp.int32, labels_ref.shape, 0)
    own = jnp.where(images == me, labels_ref[...].astype(F32), 0.0)
    own = jnp.sum(own, axis=0, keepdims=True)
    own_ids = lax.broadcasted_iota(jnp.int32, (BLK, slots), 0).astype(F32)
    same = jnp.sum(jnp.where(own_ids == own, histogram, 0.0), axis=0, keepdims=True)
    slot_ids = lax.broadcasted_iota(jnp.int32, (1, slots), 1)
    keep = jnp.where(slot_ids < blocks_ref[me] * BLK, 1.0, 0.0)
    wide[...] = jnp.zeros_like(wide)
    wide[0:1, :] = keep
    wide[1:2, :] = own
    wide[2:3, :] = keep * (same - 1.0)
    lanes_ref[...] = wide[0:8, :]
    info_ref[...] = wide[...].T


def pack_kernel(first_unit, blocks_ref, recv_ref, rep_hbm, packed, sems):
    half = lax.div(lax.axis_index("group"), PARTS)
    packed[...] = jnp.zeros_like(packed)
    units = packed.shape[0] // UNIT

    def one_image(image, place):
        odd = lax.rem(place, 2)
        first = half + odd - 2 * half * odd
        for pair in range(2):
            block = 2 * pair + first
            unit = lax.div(place + block, 2) - first_unit

            @pl.when((block < blocks_ref[image]) & (unit >= 0) & (unit < units))
            def _():
                packed[pl.ds(pl.multiple_of(unit * UNIT, UNIT), UNIT), :] = recv_ref[
                    image, pair * UNIT : (pair + 1) * UNIT, :
                ]

        return place + blocks_ref[image]

    lax.fori_loop(0, blocks_ref.shape[0], one_image, jnp.int32(0))
    copies = [
        pltpu.make_async_copy(packed, rep_hbm.at[device], sems.at[device])
        for device in range(rep_hbm.shape[0])
    ]
    for copy in copies:
        copy.start()
    for copy in copies:
        copy.wait()


def skip_kernel(blocks_ref, out_hbm):
    pass


def load_keys(valid, keys_hbm, more_hbm, keys, sems):
    units = keys_hbm.shape[1]
    more = more_hbm.shape[1]

    def copies_of(which, source, start, count, place):
        return [
            pltpu.make_async_copy(
                source.at[device, pl.ds(start, count)],
                keys.at[pl.ds(place, count), device // PARTS, device % PARTS],
                sems.at[which, device],
            )
            for device in range(2 * PARTS)
        ]

    starts = [start for start in SOON if start < units]
    waits = {}
    for which, (start, end) in enumerate(zip(starts, starts[1:] + [units])):
        copies = copies_of(which, keys_hbm, start, end - start, start)
        for copy in copies:
            copy.start()
        waits[start // 2] = copies
    last = copies_of(len(SOON), more_hbm, 0, more, units)

    @pl.when(valid > ROOM)
    def _():
        for copy in last:
            copy.start()
        for copy in last:
            copy.wait()

    return waits


def each_tile(valid, waits, visit):
    for tile in range(ROOM * BLK // TILE):
        for copy in waits.get(tile, ()):
            copy.wait()
        if (tile + 1) * TILE < ROOM * BLK:
            visit(tile)
        else:
            pl.when(valid > tile * (TILE // BLK))(functools.partial(visit, tile))

    def later(tile, carry):
        visit(tile)
        return carry

    per_tile = TILE // BLK
    lax.fori_loop(ROOM // per_tile, lax.div(valid + per_tile - 1, per_tile), later, 0)


def key_tile_of(keys, tile):
    return keys[pl.ds(2 * tile, 2)].reshape(TILE, keys.shape[-1])


def lanes_of(tile):
    start = tile * TILE
    return pl.ds(start if isinstance(start, int) else pl.multiple_of(start, TILE), TILE)


def not_own(rows, first_place, tile):
    row_ids = lax.broadcasted_iota(jnp.int32, (rows, TILE), 0)
    lane_ids = lax.broadcasted_iota(jnp.int32, (rows, TILE), 1)
    return lane_ids - row_ids != first_place * BLK - tile * TILE


def sums_kernel(
    blocks_ref, lanes_ref, own_ref, keys_hbm, more_hbm, acc_ref, send_ref, keys, sems
):
    valid = blocks_before(blocks_ref, blocks_ref.shape[0])
    waits = load_keys(valid, keys_hbm, more_hbm, keys, sems)
    first_place = blocks_before(blocks_ref, lax.axis_index("group"))
    acc_ref[...] = jnp.zeros_like(acc_ref)
    own = own_ref[...]
    lane_ids = lax.broadcasted_iota(jnp.int32, (1, TILE), 1)

    def visit(tile):
        key_tile = key_tile_of(keys, tile)
        weights = jnp.exp(dot_f32(own, key_tile, NT) * INV_TEMP)
        if not isinstance(tile, int) or (tile + 1) * TILE > blocks_ref.shape[0] * BLK:
            weights = weights * jnp.where(lane_ids < valid * BLK - tile * TILE, 1.0, 0.0)
        weights = jnp.where(not_own(own.shape[0], first_place, tile), weights, 0.0)
        acc_ref[...] += fold_lanes(weights)

    each_tile(valid, waits, visit)
    for block in range(own.shape[0] // BLK):
        rows = slice(block * BLK, (block + 1) * BLK)
        total = jnp.sum(acc_ref[rows, :].T, axis=0, keepdims=True)
        pos_count = lanes_ref[2:3, rows]
        scale = pos_count / jnp.maximum(pos_count, 1.0) / total
        for device in range(send_ref.shape[0]):
            send_ref[device, block : block + 1, :] = scale


def rows_kernel(
    blocks_ref, own_ref, info_ref, acc_ref, key_label_ref, keys_hbm, more_hbm,
    grad_ref, scale_ref, loss_ref, keys, by_class, sems,
):
    valid = blocks_before(blocks_ref, blocks_ref.shape[0])
    waits = load_keys(valid, keys_hbm, more_hbm, keys, sems)
    class_ids = lax.broadcasted_iota(jnp.int32, (BLK, TILE), 0).astype(F32)
    by_class[...] = jnp.zeros_like(by_class)

    def visit(tile):
        member = class_ids == key_label_ref[:, lanes_of(tile)]
        member = jnp.where(member, 1.0, 0.0).astype(BF16)
        by_class[...] += dot_f32(member, key_tile_of(keys, tile))

    each_tile(valid, waits, visit)
    keep = info_ref[:, 0:1]
    pos_count = info_ref[:, 2:3]
    lane_ids = lax.broadcasted_iota(jnp.int32, info_ref.shape, 1).astype(F32)
    member = jnp.where(lane_ids == info_ref[:, 1:2], 1.0, 0.0).astype(BF16)
    own = own_ref[...].astype(F32)
    others = sum(dot_f32(member, part) for part in split_bf16(by_class[...], 3)) - own
    pos_floor = jnp.maximum(pos_count, 1.0)
    total = jnp.sum(acc_ref[...], axis=1, keepdims=True)
    scale_ref[...] = jnp.broadcast_to((pos_count / pos_floor) / total, scale_ref.shape)
    grad_ref[...] = (-2.0 * keep / pos_floor) * others
    same_sum = INV_TEMP * jnp.sum(own * others, axis=1, keepdims=True)
    loss = keep * (pos_count * jnp.log(total) - same_sum) / pos_floor
    loss = jnp.sum(loss, axis=0, keepdims=True)
    loss_ref[...] = jnp.broadcast_to(loss, loss_ref.shape)


def keys_kernel(
    blocks_ref, own_ref, row_scale_ref, scales_ref, loss_ref, row_grad_hbm, unit_hbm, length_hbm, picked_hbm, class_hbm,
    keys_hbm, more_hbm, grad_ref, out_ref,
    keys, scale, acc, row_grad, unit, length, picked, sems, end_sems,
):
    valid = blocks_before(blocks_ref, blocks_ref.shape[0])
    waits = load_keys(valid, keys_hbm, more_hbm, keys, sems)
    late = [
        pltpu.make_async_copy(source, target, end_sems.at[i])
        for i, (source, target) in enumerate(
            [
                (row_grad_hbm, row_grad),
                (unit_hbm, unit),
                (length_hbm, length),
                (picked_hbm, picked),
                (class_hbm, out_ref.at[:, pl.ds(unit.shape[1], BLK)]),
            ]
        )
    ]
    for copy in late:
        copy.start()
    first_place = blocks_before(blocks_ref, lax.axis_index("group"))
    scale[...] = jnp.zeros_like(scale)
    place = jnp.int32(0)
    for image in range(blocks_ref.shape[0]):
        for block in range(scales_ref.shape[1]):
            scale[pl.ds(place + block, 1), :] = scales_ref[image, block : block + 1, :]
        place = place + blocks_ref[image]
    acc[...] = jnp.zeros_like(acc)
    own = own_ref[...]
    row_scale = row_scale_ref[:, 0:1]

    def visit(tile):
        key_tile = key_tile_of(keys, tile)
        per_tile = TILE // BLK
        key_scale = jnp.concatenate(
            [scale[pl.ds(tile * per_tile + i, 1), :] for i in range(per_tile)], axis=1
        )
        weights = jnp.exp(dot_f32(own, key_tile, NT) * INV_TEMP) * (row_scale + key_scale)
        weights = jnp.where(not_own(own.shape[0], first_place, tile), weights, 0.0)
        acc[...] += dot_f32(weights.astype(BF16), key_tile)

    each_tile(valid, waits, visit)
    for copy in late:
        copy.wait()
    grad = row_grad[...] + acc[...]
    radial = jnp.sum(unit[...] * grad, axis=1, keepdims=True)
    grad = (grad - unit[...] * radial) * length[:, 0:1]
    grad_ref[...] = grad
    width = grad.shape[1]
    out_ref[:, :width] = sum(dot_f32(picked[...], part) for part in split_bf16(grad, 2))
    last = (out_ref.shape[0], 1)
    out_ref[:, width + BLK - 1 :] = jnp.broadcast_to(loss_ref[0:1, 0:1], last)


def features_kernel(pix_ref, grad_ref, proj_ref, logits_ref, class_ref, out_ref):
    rows = out_ref.shape[0]
    slots = pix_ref.shape[1]
    ids = pl.program_id(0) * rows + lax.broadcasted_iota(jnp.int32, (rows, slots), 0)
    onehot = jnp.where(ids == pix_ref[...], 1.0, 0.0).astype(BF16)
    proj = proj_ref[...]
    total = dot_f32(logits_ref[...], class_ref[...], NT)
    for part in split_bf16(grad_ref[...], 2):
        total = total + dot_f32(dot_f32(onehot, part).astype(BF16), proj, NT)
    out_ref[...] = total.astype(BF16)


def add_kernel(classes, recv_ref, rep_hbm, total_ref, sems):
    total = recv_ref[0]
    for device in range(1, recv_ref.shape[0]):
        total = total + recv_ref[device]
    high, middle, low = split_bf16(total, 3)
    rows = lax.broadcasted_iota(jnp.int32, total.shape, 0)
    is_loss = lax.broadcasted_iota(jnp.int32, total.shape, 1) >= total.shape[1] - BLK + classes
    parts = jnp.where(rows == 1, middle.astype(F32), low.astype(F32))
    value = jnp.where(is_loss & (rows > 0), parts, high.astype(F32))
    total_ref[...] = value.astype(BF16)
    copies = [
        pltpu.make_async_copy(total_ref, rep_hbm.at[device], sems.at[device])
        for device in range(rep_hbm.shape[0])
    ]
    for copy in copies:
        copy.start()
    for copy in copies:
        copy.wait()


def end_kernel(pixels, blocks_ref, summed_ref, proj_ref, class_ref, losses_ref):
    width = proj_ref.shape[1]
    classes = class_ref.shape[1]
    summed = summed_ref[...].astype(F32)
    proj_ref[...] = summed[:, :width]
    class_ref[...] = summed[:, width : width + classes]
    groups = blocks_ref.shape[0]
    anchors = (blocks_before(blocks_ref, groups) * BLK).astype(F32)
    top = summed[:8, width:]
    rows = lax.broadcasted_iota(jnp.int32, top.shape, 0)
    lanes = lax.broadcasted_iota(jnp.int32, top.shape, 1)
    pixel_loss = jnp.sum(jnp.where((rows < 3) & (lanes == classes), top, 0.0))
    contrast = jnp.sum(jnp.where((rows < 3) & (lanes == BLK - 1), top, 0.0))
    losses_ref[0] = pixel_loss / pixels
    losses_ref[1] = contrast / anchors


SMEM = pl.BlockSpec(memory_space=pltpu.SMEM)
VMEM = pl.BlockSpec()
ANY = pl.BlockSpec(memory_space=pl.ANY)


def shape_of(shape, dtype=F32):
    return jax.ShapeDtypeStruct(shape, dtype)


def call(kernel, name, ins, outs, out_specs=None, scratch=(), flops=0, exps=0, vmem=VMEM_BYTES):
    size = sum(a.size * a.dtype.itemsize for a, _ in ins)
    size += sum(o.size * o.dtype.itemsize for o in outs)
    return pl.pallas_call(
        kernel,
        name=name,
        out_shape=outs,
        in_specs=[s for _, s in ins],
        out_specs=out_specs or [VMEM] * len(outs),
        scratch_shapes=list(scratch),
        compiler_params=pltpu.CompilerParams(vmem_limit_bytes=vmem),
        cost_estimate=pl.CostEstimate(flops=flops, bytes_accessed=size, transcendentals=exps),
    )(*[a for a, _ in ins])


def exchange(value):
    return lax.all_to_all(value, "group", 0, 0, tiled=True)


def per_device(
    features, proj_weight, class_weight, anchor_blocks, anchor_pix, anchor_label, pixel_label
):
    groups = lax.axis_size("group")
    slots = anchor_pix.shape[1]
    pixels, channels = features.shape
    classes = class_weight.shape[1]
    width = proj_weight.shape[1]
    per_image = slots // BLK
    blocks = groups * per_image
    share = channels // groups
    valid = jnp.sum(anchor_blocks)

    emb, send = call(
        pick_kernel, "pick_anchors",
        [(anchor_blocks, SMEM), (anchor_pix, VMEM), (features, ANY), (proj_weight, VMEM)],
        [shape_of((slots, width), BF16), shape_of((groups, slots // groups, width), BF16)],
        None, [pltpu.VMEM(features.shape, BF16), pltpu.SemaphoreType.DMA((4,))],
        flops=2 * slots * channels * (pixels + width),
    )
    recv = exchange(send)

    def packed(first_unit, units):
        (rep,) = call(
            functools.partial(pack_kernel, first_unit), "pack_keys",
            [(anchor_blocks, SMEM), (recv, VMEM)],
            [shape_of((groups, units * UNIT, width), BF16)], [ANY],
            [pltpu.VMEM((units * UNIT, width), BF16), pltpu.SemaphoreType.DMA((groups,))],
        )
        return rep

    units, more_units = ROOM // 2, (blocks - ROOM) // 2

    def second_exchange():
        return exchange(packed(units, more_units))

    def no_exchange():
        shape = shape_of((groups, more_units * UNIT, width), BF16)
        return call(skip_kernel, "skip_keys", [(anchor_blocks, SMEM)], [shape], [ANY])[0]

    rep = packed(0, units)
    keys = exchange(rep).reshape(groups, units, UNIT, width)
    more = lax.cond(valid > ROOM, second_exchange, no_exchange)
    more = more.reshape(groups, more_units, UNIT, width)

    labels, late_features, _ = lax.optimization_barrier((anchor_label, features, rep))
    key_label, info, lanes, unit, scale, picked_t = call(
        label_kernel, "anchor_labels",
        [(anchor_blocks, SMEM), (labels, VMEM), (anchor_pix, VMEM), (late_features, ANY),
         (proj_weight, VMEM)],
        [shape_of((1, blocks * BLK)), shape_of((slots, BLK)), shape_of((8, slots)),
         shape_of((slots, width)), shape_of((slots, BLK)), shape_of((channels, slots), BF16)],
        None,
        [pltpu.VMEM((BLK, slots), F32), pltpu.VMEM(features.shape, BF16),
         pltpu.SemaphoreType.DMA((4,))],
        vmem=LABEL_BYTES,
    )
    logits = jnp.dot(late_features, class_weight, preferred_element_type=F32)
    top_logit = jnp.max(logits, axis=1, keepdims=True)
    logsum_class = jnp.log(jnp.sum(jnp.exp(logits - top_logit), axis=1, keepdims=True)) + top_logit
    label_ids = jnp.arange(classes, dtype=jnp.int32)
    onehot = (pixel_label[:, None] == label_ids[None, :]).astype(F32)
    pixel_loss = jnp.sum(logsum_class[:, 0] - jnp.sum(onehot * logits, axis=1))
    grad_logits = (jnp.exp(logits - logsum_class) - onehot).astype(BF16)
    class_part = dot_f32(late_features, grad_logits, TN)
    tail = jnp.broadcast_to(pixel_loss, (channels, BLK - classes))
    class_part = jnp.concatenate([class_part, tail], axis=1)
    key_scratch = pltpu.VMEM((blocks // 2, 2, PARTS, UNIT, width), BF16)
    key_sems = [pltpu.SemaphoreType.DMA((len(SOON) + 1, groups))]
    pairs = slots * ROOM * BLK
    acc, sums = call(
        sums_kernel, "anchor_sums",
        [(anchor_blocks, SMEM), (lanes, VMEM), (emb, VMEM), (keys, ANY), (more, ANY)],
        [shape_of((slots, BLK)), shape_of((groups, per_image, BLK))],
        None, [key_scratch] + key_sems, flops=2 * pairs * width, exps=pairs, vmem=MID_BYTES,
    )
    scales = exchange(sums)
    row_grad, row_scale, loss = call(
        rows_kernel, "anchor_rows",
        [(anchor_blocks, SMEM), (emb, VMEM), (info, VMEM), (acc, VMEM), (key_label, VMEM),
         (keys, ANY), (more, ANY)],
        [shape_of((slots, width)), shape_of((slots, BLK)), shape_of((8, BLK))],
        None, [key_scratch, pltpu.VMEM((BLK, width), F32)] + key_sems,
        flops=2 * ROOM * BLK * BLK * width, vmem=MID_BYTES,
    )
    grad_projected, part = call(
        keys_kernel, "anchor_keys",
        [(anchor_blocks, SMEM), (emb, VMEM), (row_scale, VMEM), (scales, VMEM), (loss, VMEM), (row_grad, ANY),
         (unit, ANY), (scale, ANY), (picked_t, ANY), (class_part, ANY), (keys, ANY), (more, ANY)],
        [shape_of((slots, width)), shape_of((channels, width + BLK))],
        None,
        [key_scratch, pltpu.VMEM((blocks + 8, BLK), F32), pltpu.VMEM((slots, width), F32),
         pltpu.VMEM((slots, width), F32), pltpu.VMEM((slots, width), F32),
         pltpu.VMEM((slots, BLK), F32), pltpu.VMEM((channels, slots), BF16)]
        + key_sems + [pltpu.SemaphoreType.DMA((5,))],
        flops=4 * pairs * width, exps=pairs, vmem=MID_BYTES,
    )

    received = exchange(part.reshape(groups, share, width + BLK))
    tile = pixels // 4
    (grad_features,) = pl.pallas_call(
        features_kernel,
        name="feature_grads",
        grid=(pixels // tile,),
        out_shape=[shape_of((pixels, channels), BF16)],
        in_specs=[
            pl.BlockSpec((1, slots), lambda i: (0, 0)),
            pl.BlockSpec((slots, width), lambda i: (0, 0)),
            pl.BlockSpec((channels, width), lambda i: (0, 0)),
            pl.BlockSpec((tile, classes), lambda i: (i, 0)),
            pl.BlockSpec((channels, classes), lambda i: (0, 0)),
        ],
        out_specs=[pl.BlockSpec((tile, channels), lambda i: (i, 0))],
        compiler_params=pltpu.CompilerParams(vmem_limit_bytes=VMEM_BYTES),
        cost_estimate=pl.CostEstimate(
            flops=2 * pixels * (2 * slots * width + 2 * width * channels + classes * channels),
            bytes_accessed=4 * pixels * channels,
            transcendentals=0,
        ),
    )(anchor_pix, grad_projected, proj_weight, grad_logits, class_weight)
    (part_rep,) = call(
        functools.partial(add_kernel, classes), "add_shares", [(received, VMEM)],
        [shape_of(received.shape, BF16)], [ANY],
        [pltpu.VMEM(received.shape[1:], BF16), pltpu.SemaphoreType.DMA((groups,))],
        vmem=SMALL_BYTES,
    )
    summed = exchange(part_rep).reshape(channels, width + BLK)
    grad_proj, grad_class, losses = call(
        functools.partial(end_kernel, float(groups * pixels)), "outputs",
        [(anchor_blocks, SMEM), (summed, VMEM)],
        [shape_of((channels, width)), shape_of((channels, classes)), shape_of((2,))],
        [VMEM, VMEM, SMEM], vmem=SMALL_BYTES,
    )
    return (grad_features, grad_proj, grad_class, losses)


def solution(mesh):
    return jax.shard_map(
        per_device,
        mesh=mesh,
        in_specs=(
            P(("dp", "group"), None),
            P(),
            P("dp", None),
            P("dp"),
            P(("dp", "group"), None),
            P("dp", None),
            P(("dp", "group")),
        ),
        out_specs=(P(("dp", "group"), None), P("dp", None), P("dp", None), P("dp")),
        check_vma=False,
    )
```

```python
import functools

import jax
import jax.numpy as jnp
from jax import lax
from jax.experimental import pallas as pl
from jax.experimental.pallas import tpu as pltpu
from jax.sharding import PartitionSpec as P

BLK = 128
SOON = (0, 4, 12)
UNIT = 16
PARTS = BLK // UNIT
TILE = 1024
ROOM = 40
PAIRS = TILE // (2 * BLK)
INV_TEMP = 10.0
EXP_SCALE = INV_TEMP * 1.4426950408889634
NORM_EPS = 1e-06
VMEM_BYTES = 63 * 1024 * 1024
MID_BYTES = 40 * 1024 * 1024
LABEL_BYTES = 63 * 1024 * 1024
SMALL_BYTES = 16 * 1024 * 1024

NN = (((1,), (0,)), ((), ()))
NT = (((1,), (1,)), ((), ()))
TN = (((0,), (0,)), ((), ()))
F32 = jnp.float32
BF16 = jnp.bfloat16


def dot_f32(left, right, dims=NN):
    return lax.dot_general(left, right, dims, preferred_element_type=F32)


def split_bf16(value, count):
    parts = []
    for _ in range(count):
        parts.append(value.astype(BF16))
        value = value - parts[-1].astype(F32)
    return parts


def blocks_before(blocks_ref, image):
    total = jnp.int32(0)
    for group in range(blocks_ref.shape[0]):
        total = total + jnp.where(group < image, blocks_ref[group], 0)
    return total


def each_block(blocks_ref, visit):
    place = jnp.int32(0)
    for image in range(blocks_ref.shape[0]):
        count = blocks_ref[image]
        for block in range(4):
            pl.when(block < count)(functools.partial(visit, image, block, place + block))
        place = place + count


def fold_lanes(value):
    total = value[:, :BLK]
    for start in range(BLK, value.shape[1], BLK):
        total = total + value[:, start : start + BLK]
    return total


def column_of(row, height=BLK):
    return jnp.broadcast_to(row, (height, row.shape[1])).T[:, 0:1]


def project(picked, proj):
    projected = dot_f32(picked, proj)
    inverse = lax.rsqrt(jnp.sum(projected * projected, axis=1, keepdims=True) + NORM_EPS)
    return projected * inverse, inverse


def pick(pix_ref, features_hbm, features, sems, beside):
    slots = pix_ref.shape[1]
    step = features.shape[0] // sems.shape[0]
    copies = [
        pltpu.make_async_copy(
            features_hbm.at[pl.ds(part * step, step)],
            features.at[pl.ds(part * step, step)],
            sems.at[part],
        )
        for part in range(sems.shape[0])
    ]
    for copy in copies:
        copy.start()
    beside()
    pix = column_of(pix_ref[...].astype(F32)).astype(jnp.int32)
    lanes = lax.broadcasted_iota(jnp.int32, (slots, step), 1)
    total = jnp.zeros((slots, features.shape[1]), F32)
    for part, copy in enumerate(copies):
        onehot = jnp.where(lanes == pix - part * step, 1.0, 0.0).astype(BF16)
        copy.wait()
        total = total + dot_f32(onehot, features[part * step : (part + 1) * step, :])
    return total


def pick_kernel(
    blocks_ref, pix_ref, features_hbm, proj_ref, emb_ref, send_ref, features, sems
):
    slots = pix_ref.shape[1]
    picked = pick(pix_ref, features_hbm, features, sems, lambda: None).astype(BF16)
    unit, _ = project(picked, proj_ref[...])
    emb_ref[...] = unit.astype(BF16)
    odd = lax.rem(blocks_before(blocks_ref, lax.axis_index("group")), 2)
    for half in range(2):
        first = half + odd - 2 * half * odd
        for part in range(PARTS):
            for pair in range(slots // BLK // 2):
                start = pl.multiple_of((2 * pair + first) * BLK + part * UNIT, UNIT)
                send_ref[half * PARTS + part, pair * UNIT : (pair + 1) * UNIT, :] = emb_ref[
                    pl.ds(start, UNIT), :
                ]


def label_kernel(
    blocks_ref, labels_ref, pix_ref, features_hbm, proj_ref,
    key_label_ref, info_ref, lanes_ref, unit_ref, scale_ref, picked_ref, wide, features, sems,
):
    def labels():
        label_terms(blocks_ref, labels_ref, key_label_ref, info_ref, lanes_ref, wide)

    picked = pick(pix_ref, features_hbm, features, sems, labels)
    picked_ref[...] = picked.T.astype(BF16)
    unit, inverse = project(picked.astype(BF16), proj_ref[...])
    unit_ref[...] = unit
    scale_ref[...] = jnp.broadcast_to(info_ref[:, 0:1] * inverse, scale_ref.shape)


def label_terms(blocks_ref, labels_ref, key_label_ref, info_ref, lanes_ref, wide):
    me = lax.axis_index("group")
    slots = labels_ref.shape[1]
    key_label_ref[...] = jnp.full_like(key_label_ref, -1.0)

    def place_labels(image, block, place):
        span = pl.ds(pl.multiple_of(place * BLK, BLK), BLK)
        part = labels_ref[image : image + 1, block * BLK : (block + 1) * BLK]
        key_label_ref[:, span] = part.astype(F32)

    each_block(blocks_ref, place_labels)
    class_ids = lax.broadcasted_iota(jnp.int32, (BLK, BLK), 0).astype(F32)
    counts = jnp.zeros((BLK, BLK), F32)
    for start in range(0, key_label_ref.shape[1], BLK):
        counts = counts + jnp.where(class_ids == key_label_ref[:, start : start + BLK], 1.0, 0.0)
    histogram = jnp.sum(counts, axis=1, keepdims=True)
    images = lax.broadcasted_iota(jnp.int32, labels_ref.shape, 0)
    own = jnp.where(images == me, labels_ref[...].astype(F32), 0.0)
    own = jnp.sum(own, axis=0, keepdims=True)
    own_ids = lax.broadcasted_iota(jnp.int32, (BLK, slots), 0).astype(F32)
    same = jnp.sum(jnp.where(own_ids == own, histogram, 0.0), axis=0, keepdims=True)
    slot_ids = lax.broadcasted_iota(jnp.int32, (1, slots), 1)
    keep = jnp.where(slot_ids < blocks_ref[me] * BLK, 1.0, 0.0)
    wide[...] = jnp.zeros_like(wide)
    wide[0:1, :] = keep
    wide[1:2, :] = own
    wide[2:3, :] = keep * (same - 1.0)
    lanes_ref[...] = wide[0:8, :]
    info_ref[...] = wide[...].T


def pack_kernel(first_unit, blocks_ref, recv_ref, rep_hbm, packed, sems):
    half = lax.axis_index("group") >> (PARTS.bit_length() - 1)
    packed[...] = jnp.zeros_like(packed)
    units = packed.shape[0] // UNIT
    place = jnp.int32(0)
    for image in range(blocks_ref.shape[0]):
        first = half ^ (place & 1)
        for pair in range(2):
            block = 2 * pair + first
            unit = ((place + block) >> 1) - first_unit

            def move(unit=unit, image=image, pair=pair):
                packed[pl.ds(pl.multiple_of(unit * UNIT, UNIT), UNIT), :] = recv_ref[
                    image, pair * UNIT : (pair + 1) * UNIT, :
                ]

            pl.when((block < blocks_ref[image]) & (unit >= 0) & (unit < units))(move)
        place = place + blocks_ref[image]
    copies = [
        pltpu.make_async_copy(packed, rep_hbm.at[device], sems.at[device])
        for device in range(rep_hbm.shape[0])
    ]
    for copy in copies:
        copy.start()
    for copy in copies:
        copy.wait()


def skip_kernel(blocks_ref, out_hbm):
    pass


def load_keys(valid, keys_hbm, more_hbm, keys, sems):
    units = keys_hbm.shape[1]
    more = more_hbm.shape[1]

    def copies_of(which, source, start, count, place):
        return [
            pltpu.make_async_copy(
                source.at[device, pl.ds(start, count)],
                keys.at[pl.ds(place, count), device // PARTS, device % PARTS],
                sems.at[which, device],
            )
            for device in range(2 * PARTS)
        ]

    starts = [start for start in SOON if start < units]
    waits = {}
    for which, (start, end) in enumerate(zip(starts, starts[1:] + [units])):
        copies = copies_of(which, keys_hbm, start, end - start, start)
        for copy in copies:
            copy.start()
        waits[start // PAIRS] = copies
    last = copies_of(len(SOON), more_hbm, 0, more, units)

    @pl.when(valid > ROOM)
    def _():
        for copy in last:
            copy.start()
        for copy in last:
            copy.wait()

    return waits


def each_tile(valid, waits, visit):
    for tile in range(ROOM * BLK // TILE):
        for copy in waits.get(tile, ()):
            copy.wait()
        if (tile + 1) * TILE < ROOM * BLK:
            visit(tile)
        else:
            pl.when(valid > tile * (TILE // BLK))(functools.partial(visit, tile))

    def later(tile, carry):
        visit(tile)
        return carry

    per_tile = TILE // BLK
    lax.fori_loop(ROOM // per_tile, lax.div(valid + per_tile - 1, per_tile), later, 0)


def key_tile_of(keys, tile):
    return keys[pl.ds(PAIRS * tile, PAIRS)].reshape(TILE, keys.shape[-1])


def lanes_of(tile):
    start = tile * TILE
    return pl.ds(start if isinstance(start, int) else pl.multiple_of(start, TILE), TILE)


def not_own(rows, first_place, tile):
    row_ids = lax.broadcasted_iota(jnp.int32, (rows, TILE), 0)
    lane_ids = lax.broadcasted_iota(jnp.int32, (rows, TILE), 1)
    return lane_ids - row_ids != first_place * BLK - tile * TILE


def sums_kernel(
    blocks_ref, lanes_ref, own_ref, keys_hbm, more_hbm, acc_ref, send_ref, keys, sems
):
    valid = blocks_before(blocks_ref, blocks_ref.shape[0])
    waits = load_keys(valid, keys_hbm, more_hbm, keys, sems)
    first_place = blocks_before(blocks_ref, lax.axis_index("group"))
    acc_ref[...] = jnp.zeros_like(acc_ref)
    own = own_ref[...]
    lane_ids = lax.broadcasted_iota(jnp.int32, (1, TILE), 1)

    def visit(tile):
        key_tile = key_tile_of(keys, tile)
        weights = jnp.exp(dot_f32(own, key_tile, NT) * INV_TEMP)
        if not isinstance(tile, int) or (tile + 1) * TILE > blocks_ref.shape[0] * BLK:
            weights = weights * jnp.where(lane_ids < valid * BLK - tile * TILE, 1.0, 0.0)
        weights = jnp.where(not_own(own.shape[0], first_place, tile), weights, 0.0)
        acc_ref[...] += fold_lanes(weights)

    each_tile(valid, waits, visit)
    for block in range(own.shape[0] // BLK):
        rows = slice(block * BLK, (block + 1) * BLK)
        total = jnp.sum(acc_ref[rows, :].T, axis=0, keepdims=True)
        pos_count = lanes_ref[2:3, rows]
        scale = pos_count / jnp.maximum(pos_count, 1.0) / total
        for device in range(send_ref.shape[0]):
            send_ref[device, block : block + 1, :] = scale


def rows_kernel(
    blocks_ref, own_ref, info_ref, acc_ref, key_label_ref, keys_hbm, more_hbm,
    grad_ref, scale_ref, loss_ref, keys, by_class, sems,
):
    valid = blocks_before(blocks_ref, blocks_ref.shape[0])
    waits = load_keys(valid, keys_hbm, more_hbm, keys, sems)
    class_ids = lax.broadcasted_iota(jnp.int32, (BLK, TILE), 0).astype(F32)
    by_class[...] = jnp.zeros_like(by_class)

    def visit(tile):
        member = class_ids == key_label_ref[:, lanes_of(tile)]
        member = jnp.where(member, 1.0, 0.0).astype(BF16)
        by_class[...] += dot_f32(member, key_tile_of(keys, tile))

    each_tile(valid, waits, visit)
    keep = info_ref[:, 0:1]
    pos_count = info_ref[:, 2:3]
    lane_ids = lax.broadcasted_iota(jnp.int32, info_ref.shape, 1).astype(F32)
    member = jnp.where(lane_ids == info_ref[:, 1:2], 1.0, 0.0).astype(BF16)
    own = own_ref[...].astype(F32)
    others = sum(dot_f32(member, part) for part in split_bf16(by_class[...], 3)) - own
    pos_floor = jnp.maximum(pos_count, 1.0)
    total = jnp.sum(acc_ref[...], axis=1, keepdims=True)
    scale_ref[...] = jnp.broadcast_to((pos_count / pos_floor) / total, scale_ref.shape)
    grad_ref[...] = (-2.0 * keep / pos_floor) * others
    same_sum = INV_TEMP * jnp.sum(own * others, axis=1, keepdims=True)
    loss = keep * (pos_count * jnp.log(total) - same_sum) / pos_floor
    loss = jnp.sum(loss, axis=0, keepdims=True)
    loss_ref[...] = jnp.broadcast_to(loss, loss_ref.shape)


def keys_kernel(
    blocks_ref, own_ref, row_scale_ref, scales_ref, loss_ref, row_grad_hbm, unit_hbm, length_hbm, picked_hbm, class_hbm,
    keys_hbm, more_hbm, grad_ref, out_ref,
    keys, scale, acc, row_grad, unit, length, picked, sems, end_sems,
):
    valid = blocks_before(blocks_ref, blocks_ref.shape[0])
    waits = load_keys(valid, keys_hbm, more_hbm, keys, sems)
    late = [
        pltpu.make_async_copy(source, target, end_sems.at[i])
        for i, (source, target) in enumerate(
            [
                (row_grad_hbm, row_grad),
                (unit_hbm, unit),
                (length_hbm, length),
                (picked_hbm, picked),
                (class_hbm, out_ref.at[:, pl.ds(unit.shape[1], BLK)]),
            ]
        )
    ]
    for copy in late:
        copy.start()
    first_place = blocks_before(blocks_ref, lax.axis_index("group"))
    scale[...] = jnp.zeros_like(scale)
    place = jnp.int32(0)
    for image in range(blocks_ref.shape[0]):
        for block in range(scales_ref.shape[1]):
            scale[pl.ds(place + block, 1), :] = scales_ref[image, block : block + 1, :]
        place = place + blocks_ref[image]
    acc[...] = jnp.zeros_like(acc)
    own = own_ref[...]
    row_scale = row_scale_ref[:, 0:1]

    def visit(tile):
        key_tile = key_tile_of(keys, tile)
        per_tile = TILE // BLK
        key_scale = jnp.concatenate(
            [scale[pl.ds(tile * per_tile + i, 1), :] for i in range(per_tile)], axis=1
        )
        weights = jnp.exp(dot_f32(own, key_tile, NT) * INV_TEMP) * (row_scale + key_scale)
        weights = jnp.where(not_own(own.shape[0], first_place, tile), weights, 0.0)
        acc[...] += dot_f32(weights.astype(BF16), key_tile)

    each_tile(valid, waits, visit)
    for copy in late:
        copy.wait()
    grad = row_grad[...] + acc[...]
    radial = jnp.sum(unit[...] * grad, axis=1, keepdims=True)
    grad = (grad - unit[...] * radial) * length[:, 0:1]
    grad_ref[...] = grad
    width = grad.shape[1]
    out_ref[:, :width] = sum(dot_f32(picked[...], part) for part in split_bf16(grad, 2))
    last = (out_ref.shape[0], 1)
    out_ref[:, width + BLK - 1 :] = jnp.broadcast_to(loss_ref[0:1, 0:1], last)


def features_kernel(pix_ref, grad_ref, proj_ref, logits_ref, class_ref, out_ref):
    rows = out_ref.shape[0]
    slots = pix_ref.shape[1]
    ids = pl.program_id(0) * rows + lax.broadcasted_iota(jnp.int32, (rows, slots), 0)
    onehot = jnp.where(ids == pix_ref[...], 1.0, 0.0).astype(BF16)
    proj = proj_ref[...]
    total = dot_f32(logits_ref[...], class_ref[...], NT)
    for part in split_bf16(grad_ref[...], 2):
        total = total + dot_f32(dot_f32(onehot, part).astype(BF16), proj, NT)
    out_ref[...] = total.astype(BF16)


def add_kernel(classes, recv_ref, rep_hbm, total_ref, sems):
    total = recv_ref[0]
    for device in range(1, recv_ref.shape[0]):
        total = total + recv_ref[device]
    high, middle, low = split_bf16(total, 3)
    rows = lax.broadcasted_iota(jnp.int32, total.shape, 0)
    is_loss = lax.broadcasted_iota(jnp.int32, total.shape, 1) >= total.shape[1] - BLK + classes
    parts = jnp.where(rows == 1, middle.astype(F32), low.astype(F32))
    value = jnp.where(is_loss & (rows > 0), parts, high.astype(F32))
    total_ref[...] = value.astype(BF16)
    copies = [
        pltpu.make_async_copy(total_ref, rep_hbm.at[device], sems.at[device])
        for device in range(rep_hbm.shape[0])
    ]
    for copy in copies:
        copy.start()
    for copy in copies:
        copy.wait()


def end_kernel(pixels, blocks_ref, summed_ref, proj_ref, class_ref, losses_ref):
    width = proj_ref.shape[1]
    classes = class_ref.shape[1]
    summed = summed_ref[...].astype(F32)
    proj_ref[...] = summed[:, :width]
    class_ref[...] = summed[:, width : width + classes]
    groups = blocks_ref.shape[0]
    anchors = (blocks_before(blocks_ref, groups) * BLK).astype(F32)
    top = summed[:8, width:]
    rows = lax.broadcasted_iota(jnp.int32, top.shape, 0)
    lanes = lax.broadcasted_iota(jnp.int32, top.shape, 1)
    pixel_loss = jnp.sum(jnp.where((rows < 3) & (lanes == classes), top, 0.0))
    contrast = jnp.sum(jnp.where((rows < 3) & (lanes == BLK - 1), top, 0.0))
    losses_ref[0] = pixel_loss / pixels
    losses_ref[1] = contrast / anchors


SMEM = pl.BlockSpec(memory_space=pltpu.SMEM)
VMEM = pl.BlockSpec()
ANY = pl.BlockSpec(memory_space=pl.ANY)


def shape_of(shape, dtype=F32):
    return jax.ShapeDtypeStruct(shape, dtype)


def call(kernel, name, ins, outs, out_specs=None, scratch=(), flops=0, exps=0, vmem=VMEM_BYTES):
    size = sum(a.size * a.dtype.itemsize for a, _ in ins)
    size += sum(o.size * o.dtype.itemsize for o in outs)
    return pl.pallas_call(
        kernel,
        name=name,
        out_shape=outs,
        in_specs=[s for _, s in ins],
        out_specs=out_specs or [VMEM] * len(outs),
        scratch_shapes=list(scratch),
        compiler_params=pltpu.CompilerParams(vmem_limit_bytes=vmem),
        cost_estimate=pl.CostEstimate(flops=flops, bytes_accessed=size, transcendentals=exps),
    )(*[a for a, _ in ins])


def exchange(value):
    return lax.all_to_all(value, "group", 0, 0, tiled=True)


def per_device(
    features, proj_weight, class_weight, anchor_blocks, anchor_pix, anchor_label, pixel_label
):
    groups = lax.axis_size("group")
    slots = anchor_pix.shape[1]
    pixels, channels = features.shape
    classes = class_weight.shape[1]
    width = proj_weight.shape[1]
    per_image = slots // BLK
    blocks = groups * per_image
    share = channels // groups
    valid = jnp.sum(anchor_blocks)

    emb, send = call(
        pick_kernel, "pick_anchors",
        [(anchor_blocks, SMEM), (anchor_pix, VMEM), (features, ANY), (proj_weight, VMEM)],
        [shape_of((slots, width), BF16), shape_of((groups, slots // groups, width), BF16)],
        None, [pltpu.VMEM(features.shape, BF16), pltpu.SemaphoreType.DMA((4,))],
        flops=2 * slots * channels * (pixels + width),
    )
    recv = exchange(send)

    def packed(first_unit, units):
        (rep,) = call(
            functools.partial(pack_kernel, first_unit), "pack_keys",
            [(anchor_blocks, SMEM), (recv, VMEM)],
            [shape_of((groups, units * UNIT, width), BF16)], [ANY],
            [pltpu.VMEM((units * UNIT, width), BF16), pltpu.SemaphoreType.DMA((groups,))],
        )
        return rep

    units, more_units = ROOM // 2, (blocks - ROOM) // 2

    def second_exchange():
        return exchange(packed(units, more_units))

    def no_exchange():
        shape = shape_of((groups, more_units * UNIT, width), BF16)
        return call(skip_kernel, "skip_keys", [(anchor_blocks, SMEM)], [shape], [ANY])[0]

    rep = packed(0, units)
    keys = exchange(rep).reshape(groups, units, UNIT, width)
    more = lax.cond(valid > ROOM, second_exchange, no_exchange)
    more = more.reshape(groups, more_units, UNIT, width)

    labels, late_features, _ = lax.optimization_barrier((anchor_label, features, rep))
    key_label, info, lanes, unit, scale, picked_t = call(
        label_kernel, "anchor_labels",
        [(anchor_blocks, SMEM), (labels, VMEM), (anchor_pix, VMEM), (late_features, ANY),
         (proj_weight, VMEM)],
        [shape_of((1, blocks * BLK)), shape_of((slots, BLK)), shape_of((8, slots)),
         shape_of((slots, width)), shape_of((slots, BLK)), shape_of((channels, slots), BF16)],
        None,
        [pltpu.VMEM((BLK, slots), F32), pltpu.VMEM(features.shape, BF16),
         pltpu.SemaphoreType.DMA((4,))],
        vmem=LABEL_BYTES,
    )
    logits = jnp.dot(late_features, class_weight, preferred_element_type=F32)
    top_logit = jnp.max(logits, axis=1, keepdims=True)
    logsum_class = jnp.log(jnp.sum(jnp.exp(logits - top_logit), axis=1, keepdims=True)) + top_logit
    label_ids = jnp.arange(classes, dtype=jnp.int32)
    onehot = (pixel_label[:, None] == label_ids[None, :]).astype(F32)
    pixel_loss = jnp.sum(logsum_class[:, 0] - jnp.sum(onehot * logits, axis=1))
    grad_logits = (jnp.exp(logits - logsum_class) - onehot).astype(BF16)
    class_part = dot_f32(late_features, grad_logits, TN)
    tail = jnp.broadcast_to(pixel_loss, (channels, BLK - classes))
    class_part = jnp.concatenate([class_part, tail], axis=1)
    key_scratch = pltpu.VMEM((blocks // 2, 2, PARTS, UNIT, width), BF16)
    key_sems = [pltpu.SemaphoreType.DMA((len(SOON) + 1, groups))]
    pairs = slots * ROOM * BLK
    acc, sums = call(
        sums_kernel, "anchor_sums",
        [(anchor_blocks, SMEM), (lanes, VMEM), (emb, VMEM), (keys, ANY), (more, ANY)],
        [shape_of((slots, BLK)), shape_of((groups, per_image, BLK))],
        None, [key_scratch] + key_sems, flops=2 * pairs * width, exps=pairs, vmem=MID_BYTES,
    )
    scales = exchange(sums)
    row_grad, row_scale, loss = call(
        rows_kernel, "anchor_rows",
        [(anchor_blocks, SMEM), (emb, VMEM), (info, VMEM), (acc, VMEM), (key_label, VMEM),
         (keys, ANY), (more, ANY)],
        [shape_of((slots, width)), shape_of((slots, BLK)), shape_of((8, BLK))],
        None, [key_scratch, pltpu.VMEM((BLK, width), F32)] + key_sems,
        flops=2 * ROOM * BLK * BLK * width, vmem=MID_BYTES,
    )
    grad_projected, part = call(
        keys_kernel, "anchor_keys",
        [(anchor_blocks, SMEM), (emb, VMEM), (row_scale, VMEM), (scales, VMEM), (loss, VMEM), (row_grad, ANY),
         (unit, ANY), (scale, ANY), (picked_t, ANY), (class_part, ANY), (keys, ANY), (more, ANY)],
        [shape_of((slots, width)), shape_of((channels, width + BLK))],
        None,
        [key_scratch, pltpu.VMEM((blocks + 8, BLK), F32), pltpu.VMEM((slots, width), F32),
         pltpu.VMEM((slots, width), F32), pltpu.VMEM((slots, width), F32),
         pltpu.VMEM((slots, BLK), F32), pltpu.VMEM((channels, slots), BF16)]
        + key_sems + [pltpu.SemaphoreType.DMA((5,))],
        flops=4 * pairs * width, exps=pairs, vmem=MID_BYTES,
    )

    received = exchange(part.reshape(groups, share, width + BLK))
    tile = pixels // 4
    (grad_features,) = pl.pallas_call(
        features_kernel,
        name="feature_grads",
        grid=(pixels // tile,),
        out_shape=[shape_of((pixels, channels), BF16)],
        in_specs=[
            pl.BlockSpec((1, slots), lambda i: (0, 0)),
            pl.BlockSpec((slots, width), lambda i: (0, 0)),
            pl.BlockSpec((channels, width), lambda i: (0, 0)),
            pl.BlockSpec((tile, classes), lambda i: (i, 0)),
            pl.BlockSpec((channels, classes), lambda i: (0, 0)),
        ],
        out_specs=[pl.BlockSpec((tile, channels), lambda i: (i, 0))],
        compiler_params=pltpu.CompilerParams(vmem_limit_bytes=VMEM_BYTES),
        cost_estimate=pl.CostEstimate(
            flops=2 * pixels * (2 * slots * width + 2 * width * channels + classes * channels),
            bytes_accessed=4 * pixels * channels,
            transcendentals=0,
        ),
    )(anchor_pix, grad_projected, proj_weight, grad_logits, class_weight)
    (part_rep,) = call(
        functools.partial(add_kernel, classes), "add_shares", [(received, VMEM)],
        [shape_of(received.shape, BF16)], [ANY],
        [pltpu.VMEM(received.shape[1:], BF16), pltpu.SemaphoreType.DMA((groups,))],
        vmem=SMALL_BYTES,
    )
    summed = exchange(part_rep).reshape(channels, width + BLK)
    grad_proj, grad_class, losses = call(
        functools.partial(end_kernel, float(groups * pixels)), "outputs",
        [(anchor_blocks, SMEM), (summed, VMEM)],
        [shape_of((channels, width)), shape_of((channels, classes)), shape_of((2,))],
        [VMEM, VMEM, SMEM], vmem=SMALL_BYTES,
    )
    return (grad_features, grad_proj, grad_class, losses)


def solution(mesh):
    return jax.shard_map(
        per_device,
        mesh=mesh,
        in_specs=(
            P(("dp", "group"), None),
            P(),
            P("dp", None),
            P("dp"),
            P(("dp", "group"), None),
            P("dp", None),
            P(("dp", "group")),
        ),
        out_specs=(P(("dp", "group"), None), P("dp", None), P("dp", None), P("dp")),
        check_vma=False,
    )
```

```python
import functools

import jax
import jax.numpy as jnp
from jax import lax
from jax.experimental import pallas as pl
from jax.experimental.pallas import tpu as pltpu
from jax.sharding import PartitionSpec as P

BLK = 128
SOON = (0, 2, 8)
UNIT = 16
PARTS = BLK // UNIT
TILE = 512
ROOM = 40
INV_TEMP = 10.0
EXP_SCALE = INV_TEMP * 1.4426950408889634
NORM_EPS = 1e-06
VMEM_BYTES = 63 * 1024 * 1024
MID_BYTES = 40 * 1024 * 1024
LABEL_BYTES = 63 * 1024 * 1024
SMALL_BYTES = 16 * 1024 * 1024

NN = (((1,), (0,)), ((), ()))
NT = (((1,), (1,)), ((), ()))
TN = (((0,), (0,)), ((), ()))
F32 = jnp.float32
BF16 = jnp.bfloat16


def dot_f32(left, right, dims=NN):
    return lax.dot_general(left, right, dims, preferred_element_type=F32)


def split_bf16(value, count):
    parts = []
    for _ in range(count):
        parts.append(value.astype(BF16))
        value = value - parts[-1].astype(F32)
    return parts


def blocks_before(blocks_ref, image):
    total = jnp.int32(0)
    for group in range(blocks_ref.shape[0]):
        total = total + jnp.where(group < image, blocks_ref[group], 0)
    return total


def each_block(blocks_ref, visit):
    place = jnp.int32(0)
    for image in range(blocks_ref.shape[0]):
        count = blocks_ref[image]
        for block in range(4):
            pl.when(block < count)(functools.partial(visit, image, block, place + block))
        place = place + count


def fold_lanes(value):
    total = value[:, :BLK]
    for start in range(BLK, value.shape[1], BLK):
        total = total + value[:, start : start + BLK]
    return total


def column_of(row, height=BLK):
    return jnp.broadcast_to(row, (height, row.shape[1])).T[:, 0:1]


def project(picked, proj):
    projected = dot_f32(picked, proj)
    inverse = lax.rsqrt(jnp.sum(projected * projected, axis=1, keepdims=True) + NORM_EPS)
    return projected * inverse, inverse


def pick(pix_ref, features_hbm, features, sems, beside):
    slots = pix_ref.shape[1]
    step = features.shape[0] // sems.shape[0]
    copies = [
        pltpu.make_async_copy(
            features_hbm.at[pl.ds(part * step, step)],
            features.at[pl.ds(part * step, step)],
            sems.at[part],
        )
        for part in range(sems.shape[0])
    ]
    for copy in copies:
        copy.start()
    beside()
    pix = column_of(pix_ref[...].astype(F32)).astype(jnp.int32)
    lanes = lax.broadcasted_iota(jnp.int32, (slots, step), 1)
    total = jnp.zeros((slots, features.shape[1]), F32)
    for part, copy in enumerate(copies):
        onehot = jnp.where(lanes == pix - part * step, 1.0, 0.0).astype(BF16)
        copy.wait()
        total = total + dot_f32(onehot, features[part * step : (part + 1) * step, :])
    return total


def pick_kernel(
    blocks_ref, pix_ref, features_hbm, proj_ref, emb_ref, send_ref, features, sems
):
    slots = pix_ref.shape[1]
    picked = pick(pix_ref, features_hbm, features, sems, lambda: None).astype(BF16)
    unit, _ = project(picked, proj_ref[...])
    emb_ref[...] = unit.astype(BF16)
    odd = lax.rem(blocks_before(blocks_ref, lax.axis_index("group")), 2)
    for half in range(2):
        first = half + odd - 2 * half * odd
        for part in range(PARTS):
            for pair in range(slots // BLK // 2):
                start = pl.multiple_of((2 * pair + first) * BLK + part * UNIT, UNIT)
                send_ref[half * PARTS + part, pair * UNIT : (pair + 1) * UNIT, :] = emb_ref[
                    pl.ds(start, UNIT), :
                ]


def label_kernel(
    blocks_ref, labels_ref, pix_ref, features_hbm, proj_ref,
    key_label_ref, info_ref, lanes_ref, unit_ref, scale_ref, picked_ref, wide, features, sems,
):
    def labels():
        label_terms(blocks_ref, labels_ref, key_label_ref, info_ref, lanes_ref, wide)

    picked = pick(pix_ref, features_hbm, features, sems, labels)
    picked_ref[...] = picked.T.astype(BF16)
    unit, inverse = project(picked.astype(BF16), proj_ref[...])
    unit_ref[...] = unit
    scale_ref[...] = jnp.broadcast_to(info_ref[:, 0:1] * inverse, scale_ref.shape)


def label_terms(blocks_ref, labels_ref, key_label_ref, info_ref, lanes_ref, wide):
    me = lax.axis_index("group")
    slots = labels_ref.shape[1]
    key_label_ref[...] = jnp.full_like(key_label_ref, -1.0)

    def place_labels(image, block, place):
        span = pl.ds(pl.multiple_of(place * BLK, BLK), BLK)
        part = labels_ref[image : image + 1, block * BLK : (block + 1) * BLK]
        key_label_ref[:, span] = part.astype(F32)

    each_block(blocks_ref, place_labels)
    class_ids = lax.broadcasted_iota(jnp.int32, (BLK, BLK), 0).astype(F32)
    counts = jnp.zeros((BLK, BLK), F32)
    for start in range(0, key_label_ref.shape[1], BLK):
        counts = counts + jnp.where(class_ids == key_label_ref[:, start : start + BLK], 1.0, 0.0)
    histogram = jnp.sum(counts, axis=1, keepdims=True)
    images = lax.broadcasted_iota(jnp.int32, labels_ref.shape, 0)
    own = jnp.where(images == me, labels_ref[...].astype(F32), 0.0)
    own = jnp.sum(own, axis=0, keepdims=True)
    own_ids = lax.broadcasted_iota(jnp.int32, (BLK, slots), 0).astype(F32)
    same = jnp.sum(jnp.where(own_ids == own, histogram, 0.0), axis=0, keepdims=True)
    slot_ids = lax.broadcasted_iota(jnp.int32, (1, slots), 1)
    keep = jnp.where(slot_ids < blocks_ref[me] * BLK, 1.0, 0.0)
    wide[...] = jnp.zeros_like(wide)
    wide[0:1, :] = keep
    wide[1:2, :] = own
    wide[2:3, :] = keep * (same - 1.0)
    lanes_ref[...] = wide[0:8, :]
    info_ref[...] = wide[...].T


def pack_kernel(first_unit, blocks_ref, recv_ref, rep_hbm, packed, sems):
    half = lax.axis_index("group") >> (PARTS.bit_length() - 1)
    packed[...] = jnp.zeros_like(packed)
    units = packed.shape[0] // UNIT
    place = jnp.int32(0)
    for image in range(blocks_ref.shape[0]):
        first = half ^ (place & 1)
        for pair in range(2):
            block = 2 * pair + first
            unit = ((place + block) >> 1) - first_unit

            def move(unit=unit, image=image, pair=pair):
                packed[pl.ds(pl.multiple_of(unit * UNIT, UNIT), UNIT), :] = recv_ref[
                    image, pair * UNIT : (pair + 1) * UNIT, :
                ]

            pl.when((block < blocks_ref[image]) & (unit >= 0) & (unit < units))(move)
        place = place + blocks_ref[image]
    copies = [
        pltpu.make_async_copy(packed, rep_hbm.at[device], sems.at[device])
        for device in range(rep_hbm.shape[0])
    ]
    for copy in copies:
        copy.start()
    for copy in copies:
        copy.wait()


def skip_kernel(blocks_ref, out_hbm):
    pass


def load_keys(valid, keys_hbm, more_hbm, keys, sems):
    units = keys_hbm.shape[1]
    more = more_hbm.shape[1]

    def copies_of(which, source, start, count, place):
        return [
            pltpu.make_async_copy(
                source.at[device, pl.ds(start, count)],
                keys.at[pl.ds(place, count), device // PARTS, device % PARTS],
                sems.at[which, device],
            )
            for device in range(2 * PARTS)
        ]

    starts = [start for start in SOON if start < units]
    waits = {}
    for which, (start, end) in enumerate(zip(starts, starts[1:] + [units])):
        copies = copies_of(which, keys_hbm, start, end - start, start)
        for copy in copies:
            copy.start()
        waits[start // 2] = copies
    last = copies_of(len(SOON), more_hbm, 0, more, units)

    @pl.when(valid > ROOM)
    def _():
        for copy in last:
            copy.start()
        for copy in last:
            copy.wait()

    return waits


def each_tile(valid, waits, visit):
    for tile in range(ROOM * BLK // TILE):
        for copy in waits.get(tile, ()):
            copy.wait()
        if (tile + 1) * TILE < ROOM * BLK:
            visit(tile)
        else:
            pl.when(valid > tile * (TILE // BLK))(functools.partial(visit, tile))

    def later(tile, carry):
        visit(tile)
        return carry

    per_tile = TILE // BLK
    lax.fori_loop(ROOM // per_tile, lax.div(valid + per_tile - 1, per_tile), later, 0)


def key_tile_of(keys, tile):
    return keys[pl.ds(2 * tile, 2)].reshape(TILE, keys.shape[-1])


def lanes_of(tile):
    start = tile * TILE
    return pl.ds(start if isinstance(start, int) else pl.multiple_of(start, TILE), TILE)


def not_own(rows, first_place, tile):
    row_ids = lax.broadcasted_iota(jnp.int32, (rows, TILE), 0)
    lane_ids = lax.broadcasted_iota(jnp.int32, (rows, TILE), 1)
    return lane_ids - row_ids != first_place * BLK - tile * TILE


def sums_kernel(
    blocks_ref, lanes_ref, own_ref, keys_hbm, more_hbm, acc_ref, send_ref, keys, sems
):
    valid = blocks_before(blocks_ref, blocks_ref.shape[0])
    waits = load_keys(valid, keys_hbm, more_hbm, keys, sems)
    first_place = blocks_before(blocks_ref, lax.axis_index("group"))
    acc_ref[...] = jnp.zeros_like(acc_ref)
    own = own_ref[...]
    lane_ids = lax.broadcasted_iota(jnp.int32, (1, TILE), 1)

    def visit(tile):
        key_tile = key_tile_of(keys, tile)
        weights = jnp.exp(dot_f32(own, key_tile, NT) * INV_TEMP)
        if not isinstance(tile, int) or (tile + 1) * TILE > blocks_ref.shape[0] * BLK:
            weights = weights * jnp.where(lane_ids < valid * BLK - tile * TILE, 1.0, 0.0)
        weights = jnp.where(not_own(own.shape[0], first_place, tile), weights, 0.0)
        acc_ref[...] += fold_lanes(weights)

    each_tile(valid, waits, visit)
    for block in range(own.shape[0] // BLK):
        rows = slice(block * BLK, (block + 1) * BLK)
        total = jnp.sum(acc_ref[rows, :].T, axis=0, keepdims=True)
        pos_count = lanes_ref[2:3, rows]
        scale = pos_count / jnp.maximum(pos_count, 1.0) / total
        for device in range(send_ref.shape[0]):
            send_ref[device, block : block + 1, :] = scale


def rows_kernel(
    blocks_ref, own_ref, info_ref, acc_ref, key_label_ref, keys_hbm, more_hbm,
    grad_ref, scale_ref, loss_ref, keys, by_class, sems,
):
    valid = blocks_before(blocks_ref, blocks_ref.shape[0])
    waits = load_keys(valid, keys_hbm, more_hbm, keys, sems)
    class_ids = lax.broadcasted_iota(jnp.int32, (BLK, TILE), 0).astype(F32)
    by_class[...] = jnp.zeros_like(by_class)

    def visit(tile):
        member = class_ids == key_label_ref[:, lanes_of(tile)]
        member = jnp.where(member, 1.0, 0.0).astype(BF16)
        by_class[...] += dot_f32(member, key_tile_of(keys, tile))

    each_tile(valid, waits, visit)
    keep = info_ref[:, 0:1]
    pos_count = info_ref[:, 2:3]
    lane_ids = lax.broadcasted_iota(jnp.int32, info_ref.shape, 1).astype(F32)
    member = jnp.where(lane_ids == info_ref[:, 1:2], 1.0, 0.0).astype(BF16)
    own = own_ref[...].astype(F32)
    others = sum(dot_f32(member, part) for part in split_bf16(by_class[...], 3)) - own
    pos_floor = jnp.maximum(pos_count, 1.0)
    total = jnp.sum(acc_ref[...], axis=1, keepdims=True)
    scale_ref[...] = jnp.broadcast_to((pos_count / pos_floor) / total, scale_ref.shape)
    grad_ref[...] = (-2.0 * keep / pos_floor) * others
    same_sum = INV_TEMP * jnp.sum(own * others, axis=1, keepdims=True)
    loss = keep * (pos_count * jnp.log(total) - same_sum) / pos_floor
    loss = jnp.sum(loss, axis=0, keepdims=True)
    loss_ref[...] = jnp.broadcast_to(loss, loss_ref.shape)


def keys_kernel(
    blocks_ref, own_ref, row_scale_ref, scales_ref, loss_ref, row_grad_hbm, unit_hbm, length_hbm, picked_hbm, class_hbm,
    keys_hbm, more_hbm, grad_ref, out_ref,
    keys, scale, acc, row_grad, unit, length, picked, sems, end_sems,
):
    valid = blocks_before(blocks_ref, blocks_ref.shape[0])
    waits = load_keys(valid, keys_hbm, more_hbm, keys, sems)
    late = [
        pltpu.make_async_copy(source, target, end_sems.at[i])
        for i, (source, target) in enumerate(
            [
                (row_grad_hbm, row_grad),
                (unit_hbm, unit),
                (length_hbm, length),
                (picked_hbm, picked),
                (class_hbm, out_ref.at[:, pl.ds(unit.shape[1], BLK)]),
            ]
        )
    ]
    for copy in late:
        copy.start()
    first_place = blocks_before(blocks_ref, lax.axis_index("group"))
    scale[...] = jnp.zeros_like(scale)
    place = jnp.int32(0)
    for image in range(blocks_ref.shape[0]):
        for block in range(scales_ref.shape[1]):
            scale[pl.ds(place + block, 1), :] = scales_ref[image, block : block + 1, :]
        place = place + blocks_ref[image]
    acc[...] = jnp.zeros_like(acc)
    own = own_ref[...]
    row_scale = row_scale_ref[:, 0:1]

    def visit(tile):
        key_tile = key_tile_of(keys, tile)
        per_tile = TILE // BLK
        key_scale = jnp.concatenate(
            [scale[pl.ds(tile * per_tile + i, 1), :] for i in range(per_tile)], axis=1
        )
        weights = jnp.exp(dot_f32(own, key_tile, NT) * INV_TEMP) * (row_scale + key_scale)
        weights = jnp.where(not_own(own.shape[0], first_place, tile), weights, 0.0)
        acc[...] += dot_f32(weights.astype(BF16), key_tile)

    each_tile(valid, waits, visit)
    for copy in late:
        copy.wait()
    grad = row_grad[...] + acc[...]
    radial = jnp.sum(unit[...] * grad, axis=1, keepdims=True)
    grad = (grad - unit[...] * radial) * length[:, 0:1]
    grad_ref[...] = grad
    width = grad.shape[1]
    out_ref[:, :width] = sum(dot_f32(picked[...], part) for part in split_bf16(grad, 2))
    last = (out_ref.shape[0], 1)
    out_ref[:, width + BLK - 1 :] = jnp.broadcast_to(loss_ref[0:1, 0:1], last)


def features_kernel(pix_ref, grad_ref, proj_ref, logits_ref, class_ref, out_ref):
    rows = out_ref.shape[0]
    slots = pix_ref.shape[1]
    ids = pl.program_id(0) * rows + lax.broadcasted_iota(jnp.int32, (rows, slots), 0)
    onehot = jnp.where(ids == pix_ref[...], 1.0, 0.0).astype(BF16)
    proj = proj_ref[...]
    total = dot_f32(logits_ref[...], class_ref[...], NT)
    for part in split_bf16(grad_ref[...], 2):
        total = total + dot_f32(dot_f32(onehot, part).astype(BF16), proj, NT)
    out_ref[...] = total.astype(BF16)


def add_kernel(classes, recv_ref, rep_hbm, total_ref, sems):
    total = recv_ref[0]
    for device in range(1, recv_ref.shape[0]):
        total = total + recv_ref[device]
    high, middle, low = split_bf16(total, 3)
    rows = lax.broadcasted_iota(jnp.int32, total.shape, 0)
    is_loss = lax.broadcasted_iota(jnp.int32, total.shape, 1) >= total.shape[1] - BLK + classes
    parts = jnp.where(rows == 1, middle.astype(F32), low.astype(F32))
    value = jnp.where(is_loss & (rows > 0), parts, high.astype(F32))
    total_ref[...] = value.astype(BF16)
    copies = [
        pltpu.make_async_copy(total_ref, rep_hbm.at[device], sems.at[device])
        for device in range(rep_hbm.shape[0])
    ]
    for copy in copies:
        copy.start()
    for copy in copies:
        copy.wait()


def end_kernel(pixels, blocks_ref, summed_ref, proj_ref, class_ref, losses_ref):
    width = proj_ref.shape[1]
    classes = class_ref.shape[1]
    summed = summed_ref[...].astype(F32)
    proj_ref[...] = summed[:, :width]
    class_ref[...] = summed[:, width : width + classes]
    groups = blocks_ref.shape[0]
    anchors = (blocks_before(blocks_ref, groups) * BLK).astype(F32)
    top = summed[:8, width:]
    rows = lax.broadcasted_iota(jnp.int32, top.shape, 0)
    lanes = lax.broadcasted_iota(jnp.int32, top.shape, 1)
    pixel_loss = jnp.sum(jnp.where((rows < 3) & (lanes == classes), top, 0.0))
    contrast = jnp.sum(jnp.where((rows < 3) & (lanes == BLK - 1), top, 0.0))
    losses_ref[0] = pixel_loss / pixels
    losses_ref[1] = contrast / anchors


SMEM = pl.BlockSpec(memory_space=pltpu.SMEM)
VMEM = pl.BlockSpec()
ANY = pl.BlockSpec(memory_space=pl.ANY)


def shape_of(shape, dtype=F32):
    return jax.ShapeDtypeStruct(shape, dtype)


def call(kernel, name, ins, outs, out_specs=None, scratch=(), flops=0, exps=0, vmem=VMEM_BYTES):
    size = sum(a.size * a.dtype.itemsize for a, _ in ins)
    size += sum(o.size * o.dtype.itemsize for o in outs)
    return pl.pallas_call(
        kernel,
        name=name,
        out_shape=outs,
        in_specs=[s for _, s in ins],
        out_specs=out_specs or [VMEM] * len(outs),
        scratch_shapes=list(scratch),
        compiler_params=pltpu.CompilerParams(vmem_limit_bytes=vmem),
        cost_estimate=pl.CostEstimate(flops=flops, bytes_accessed=size, transcendentals=exps),
    )(*[a for a, _ in ins])


def exchange(value):
    return lax.all_to_all(value, "group", 0, 0, tiled=True)


def per_device(
    features, proj_weight, class_weight, anchor_blocks, anchor_pix, anchor_label, pixel_label
):
    groups = lax.axis_size("group")
    slots = anchor_pix.shape[1]
    pixels, channels = features.shape
    classes = class_weight.shape[1]
    width = proj_weight.shape[1]
    per_image = slots // BLK
    blocks = groups * per_image
    share = channels // groups
    valid = jnp.sum(anchor_blocks)

    emb, send = call(
        pick_kernel, "pick_anchors",
        [(anchor_blocks, SMEM), (anchor_pix, VMEM), (features, ANY), (proj_weight, VMEM)],
        [shape_of((slots, width), BF16), shape_of((groups, slots // groups, width), BF16)],
        None, [pltpu.VMEM(features.shape, BF16), pltpu.SemaphoreType.DMA((4,))],
        flops=2 * slots * channels * (pixels + width),
    )
    recv = exchange(send)

    def packed(first_unit, units):
        (rep,) = call(
            functools.partial(pack_kernel, first_unit), "pack_keys",
            [(anchor_blocks, SMEM), (recv, VMEM)],
            [shape_of((groups, units * UNIT, width), BF16)], [ANY],
            [pltpu.VMEM((units * UNIT, width), BF16), pltpu.SemaphoreType.DMA((groups,))],
        )
        return rep

    units, more_units = ROOM // 2, (blocks - ROOM) // 2

    def second_exchange():
        return exchange(packed(units, more_units))

    def no_exchange():
        shape = shape_of((groups, more_units * UNIT, width), BF16)
        return call(skip_kernel, "skip_keys", [(anchor_blocks, SMEM)], [shape], [ANY])[0]

    rep = packed(0, units)
    keys = exchange(rep).reshape(groups, units, UNIT, width)
    more = lax.cond(valid > ROOM, second_exchange, no_exchange)
    more = more.reshape(groups, more_units, UNIT, width)

    labels, late_features, _ = lax.optimization_barrier((anchor_label, features, rep))
    key_label, info, lanes, unit, scale, picked_t = call(
        label_kernel, "anchor_labels",
        [(anchor_blocks, SMEM), (labels, VMEM), (anchor_pix, VMEM), (late_features, ANY),
         (proj_weight, VMEM)],
        [shape_of((1, blocks * BLK)), shape_of((slots, BLK)), shape_of((8, slots)),
         shape_of((slots, width)), shape_of((slots, BLK)), shape_of((channels, slots), BF16)],
        None,
        [pltpu.VMEM((BLK, slots), F32), pltpu.VMEM(features.shape, BF16),
         pltpu.SemaphoreType.DMA((4,))],
        vmem=LABEL_BYTES,
    )
    logits = jnp.dot(late_features, class_weight, preferred_element_type=F32)
    top_logit = jnp.max(logits, axis=1, keepdims=True)
    logsum_class = jnp.log(jnp.sum(jnp.exp(logits - top_logit), axis=1, keepdims=True)) + top_logit
    label_ids = jnp.arange(classes, dtype=jnp.int32)
    onehot = (pixel_label[:, None] == label_ids[None, :]).astype(F32)
    pixel_loss = jnp.sum(logsum_class[:, 0] - jnp.sum(onehot * logits, axis=1))
    grad_logits = (jnp.exp(logits - logsum_class) - onehot).astype(BF16)
    class_part = dot_f32(late_features, grad_logits, TN)
    tail = jnp.broadcast_to(pixel_loss, (channels, BLK - classes))
    class_part = jnp.concatenate([class_part, tail], axis=1)
    key_scratch = pltpu.VMEM((blocks // 2, 2, PARTS, UNIT, width), BF16)
    key_sems = [pltpu.SemaphoreType.DMA((len(SOON) + 1, groups))]
    pairs = slots * ROOM * BLK
    acc, sums = call(
        sums_kernel, "anchor_sums",
        [(anchor_blocks, SMEM), (lanes, VMEM), (emb, VMEM), (keys, ANY), (more, ANY)],
        [shape_of((slots, BLK)), shape_of((groups, per_image, BLK))],
        None, [key_scratch] + key_sems, flops=2 * pairs * width, exps=pairs, vmem=MID_BYTES,
    )
    scales = exchange(sums)
    row_grad, row_scale, loss = call(
        rows_kernel, "anchor_rows",
        [(anchor_blocks, SMEM), (emb, VMEM), (info, VMEM), (acc, VMEM), (key_label, VMEM),
         (keys, ANY), (more, ANY)],
        [shape_of((slots, width)), shape_of((slots, BLK)), shape_of((8, BLK))],
        None, [key_scratch, pltpu.VMEM((BLK, width), F32)] + key_sems,
        flops=2 * ROOM * BLK * BLK * width, vmem=MID_BYTES,
    )
    grad_projected, part = call(
        keys_kernel, "anchor_keys",
        [(anchor_blocks, SMEM), (emb, VMEM), (row_scale, VMEM), (scales, VMEM), (loss, VMEM), (row_grad, ANY),
         (unit, ANY), (scale, ANY), (picked_t, ANY), (class_part, ANY), (keys, ANY), (more, ANY)],
        [shape_of((slots, width)), shape_of((channels, width + BLK))],
        None,
        [key_scratch, pltpu.VMEM((blocks + 8, BLK), F32), pltpu.VMEM((slots, width), F32),
         pltpu.VMEM((slots, width), F32), pltpu.VMEM((slots, width), F32),
         pltpu.VMEM((slots, BLK), F32), pltpu.VMEM((channels, slots), BF16)]
        + key_sems + [pltpu.SemaphoreType.DMA((5,))],
        flops=4 * pairs * width, exps=pairs, vmem=MID_BYTES,
    )

    received = exchange(part.reshape(groups, share, width + BLK))
    tile = pixels // 4
    (grad_features,) = pl.pallas_call(
        features_kernel,
        name="feature_grads",
        grid=(pixels // tile,),
        out_shape=[shape_of((pixels, channels), BF16)],
        in_specs=[
            pl.BlockSpec((1, slots), lambda i: (0, 0)),
            pl.BlockSpec((slots, width), lambda i: (0, 0)),
            pl.BlockSpec((channels, width), lambda i: (0, 0)),
            pl.BlockSpec((tile, classes), lambda i: (i, 0)),
            pl.BlockSpec((channels, classes), lambda i: (0, 0)),
        ],
        out_specs=[pl.BlockSpec((tile, channels), lambda i: (i, 0))],
        compiler_params=pltpu.CompilerParams(vmem_limit_bytes=VMEM_BYTES),
        cost_estimate=pl.CostEstimate(
            flops=2 * pixels * (2 * slots * width + 2 * width * channels + classes * channels),
            bytes_accessed=4 * pixels * channels,
            transcendentals=0,
        ),
    )(anchor_pix, grad_projected, proj_weight, grad_logits, class_weight)
    (part_rep,) = call(
        functools.partial(add_kernel, classes), "add_shares", [(received, VMEM)],
        [shape_of(received.shape, BF16)], [ANY],
        [pltpu.VMEM(received.shape[1:], BF16), pltpu.SemaphoreType.DMA((groups,))],
        vmem=SMALL_BYTES,
    )
    summed = exchange(part_rep).reshape(channels, width + BLK)
    grad_proj, grad_class, losses = call(
        functools.partial(end_kernel, float(groups * pixels)), "outputs",
        [(anchor_blocks, SMEM), (summed, VMEM)],
        [shape_of((channels, width)), shape_of((channels, classes)), shape_of((2,))],
        [VMEM, VMEM, SMEM], vmem=SMALL_BYTES,
    )
    return (grad_features, grad_proj, grad_class, losses)


def solution(mesh):
    return jax.shard_map(
        per_device,
        mesh=mesh,
        in_specs=(
            P(("dp", "group"), None),
            P(),
            P("dp", None),
            P("dp"),
            P(("dp", "group"), None),
            P("dp", None),
            P(("dp", "group")),
        ),
        out_specs=(P(("dp", "group"), None), P("dp", None), P("dp", None), P("dp")),
        check_vma=False,
    )
```
